32 devices in a mesh: dp: 8 (over y, x, core), expert: 4 (over z).
Axes of the slice: x: 2, y: 2, z: 4, core: 2. Of those that a mesh axis runs over, the one named last changes fastest.
Arguments:
- tokens: bfloat16 [1024, 2048], P(('dp', 'expert')), may hold values from -6 to 6
- gates: bfloat16 [1024, 2], P(('dp', 'expert')), may hold values from 0.019897461 to 0.5
- routes: int32 [1024, 2], P(('dp', 'expert')), may hold values from 0 to 3, all different within a row; in each aligned block of 32 rows (0 to 31, 32 to 63, ...) at most 24 rows name the same one
- cotangent: bfloat16 [1024, 2048], P(('dp', 'expert')), may hold values from -6 to 6
- up_weight: bfloat16 [4, 2048, 768], P('expert'), may hold values from -0.125 to 0.125
- down_weight: bfloat16 [4, 768, 2048], P('expert'), may hold values from -0.21875 to 0.21875
Outputs:
- mixed: bfloat16 [1024, 2048], P(('dp', 'expert'))
- grad_tokens: bfloat16 [1024, 2048], P(('dp', 'expert'))
- grad_down: float32 [4, 384, 1024], P('expert', 'dp')
The draws below stay inside these ranges and needn't reach their ends.
Inputs may be any that keep to these rules, and one draw needn't show every extreme that they name: `routes`: each token names 2 different experts; among the tokens of one device no expert is named by more than 24 tokens, and in every draw some device's tokens name some expert exactly 24 times.
All inputs are finite; a program needn't handle non-finite values.
Results may differ from the reference program's by a relative error of at most 0.0066.
Values may be sent and summed in bfloat16 or wider, within the bound.
A program may use at most 64 MiB of HBM per device.

```python
import math
import jax
import jax.numpy as jnp
import numpy as np
from jax import lax

D = 2048
FF = 768
FW = 384
DW = 1024
TOK_DEV = 32
EXPERTS = 4
TOP = 2
SRC_CAP = 24
TOKENS = 1024


def shard_levels(stream_key, shape, split, smallest, largest):
    gain = 1.0
    for dim, shards_of in split:
        heights = jax.random.uniform(jax.random.fold_in(jax.random.fold_in(stream_key, 6), dim), (shards_of,), jnp.float32, smallest / len(split), largest / len(split))
        gain = gain * jnp.repeat(jnp.exp(heights), shape[dim] // shards_of).reshape((-1,) + (1,) * (len(shape) - 1 - dim))
    return gain


def shared_out(key, own, number, rows, amount, top, bound, lean):
    order = jax.random.permutation(key, amount)
    crowded, common = portions_of(amount, rows * top, bound, lean, True), portions_of(amount, rows * top, bound, lean, False)
    places = jnp.arange(amount)

    def named(tallies, turn):
        used = int((tallies > 0).sum())
        fixed = max(1, used // 4)
        shifted = fixed + (places - fixed + turn * (used - fixed)) % max(1, amount - fixed)
        return jnp.zeros((amount,), jnp.int32).at[order[jnp.where(places < fixed, places, shifted)]].set(jnp.asarray(tallies, jnp.int32))

    tallies = jnp.where(number % 4 == 0, named(crowded, number // 4), named(common, number - number // 4 - 1))
    mixed = jax.random.permutation(jax.random.fold_in(own, 3), amount)
    donor, receiver = mixed[0:amount // 2 * 2:2], mixed[1:amount // 2 * 2:2]
    margin = jnp.minimum(tallies[donor] - 1, bound - tallies[receiver]) // 2
    margin = jnp.where((donor == order[0]) | (receiver == order[0]) | (tallies[receiver] == 0), 0, jnp.maximum(margin, 0))
    shifted = jax.random.randint(jax.random.fold_in(own, 4), (amount // 2,), 0, 1 << 20) % (margin + 1)
    tallies = tallies.at[donor].add(-shifted).at[receiver].add(shifted)
    items = jnp.searchsorted(jnp.cumsum(tallies), jnp.arange(rows * top), side="right").astype(jnp.int32)
    listing = items.reshape(top, rows).T
    listing = listing[jax.random.permutation(jax.random.fold_in(own, 1), rows)]
    turn = jax.random.randint(jax.random.fold_in(own, 2), (rows, 1), 0, top)
    return jnp.take_along_axis(listing, (jnp.arange(top)[None, :] + turn) % top, axis=1)


def portions_of(amount, total, limit, slope, full):
    weights = [(1 << 20) // math.isqrt(grade ** slope) + 1 for grade in range(1, amount + 1)]
    largest = limit if full else min(limit, max(-(-total // amount), total * weights[0] // sum(weights)))
    least = 1 if total - largest >= amount - 1 else 0
    counts, rest = [largest] + [least] * (amount - 1), total - largest - least * (amount - 1)
    while rest > 0:
        movable = [i for i in range(1, amount) if counts[i] < largest] or [i for i in range(1, amount) if counts[i] < limit]
        whole, budget = sum([weights[i] for i in movable]), rest
        for i in movable:
            addition = min(limit - counts[i], max(1, budget * weights[i] // whole), rest)
            counts[i] = counts[i] + addition
            rest = rest - addition
    return np.array(counts)


def bell_draw(rng, shape, scale, limit, cuts=(), held_as=jnp.bfloat16):
    entries = scale * jax.random.normal(rng, shape, jnp.float32)
    if cuts:
        entries = entries * shard_levels(rng, shape, cuts, -0.22, 0.18)
    return jnp.clip(entries, -limit, limit).astype(held_as)


def setup_inputs(seed: int = 0) -> dict:
    streams_of = jax.random.split(jax.random.key(seed), 7)
    tokens = bell_draw(streams_of[0], (TOKENS, D), 1.0, 6.0, ((0, 32),))
    gates = jnp.clip(jnp.exp(math.log(0.5) - 3.224016 * jax.random.uniform(streams_of[1], (TOKENS, TOP), jnp.float32) ** shard_levels(streams_of[1], (TOKENS, TOP), ((0, 32),), -0.2, 0.2)), 0.019897461, 0.5).astype(jnp.bfloat16)
    routes_keys = jax.random.split(jax.random.fold_in(streams_of[2], 1), TOKENS // TOK_DEV)
    routes_turns = jax.random.permutation(jax.random.fold_in(streams_of[2], 3), TOKENS // TOK_DEV)
    routes = jax.vmap(lambda own, number: shared_out(jax.random.fold_in(streams_of[2], 2), own, number, TOK_DEV, EXPERTS, TOP, SRC_CAP, 2))(routes_keys, routes_turns).reshape((TOKENS, TOP))
    cotangent = bell_draw(streams_of[3], (TOKENS, D), 1.0, 6.0, ((0, 32),))
    up_weight = bell_draw(streams_of[4], (EXPERTS, D, FF), D ** -0.5, 0.125, ((0, 4),))
    down_weight = bell_draw(streams_of[5], (EXPERTS, FF, D), FF ** -0.5, 0.21875, ((0, 4),))
    return dict(tokens=tokens, gates=gates, routes=routes, cotangent=cotangent, up_weight=up_weight, down_weight=down_weight)


def reference(tokens, gates, routes, cotangent, up_weight, down_weight):
    blocks = TOKENS // TOK_DEV
    tok_blocks = tokens.reshape(blocks, TOK_DEV, D).astype(jnp.float32)
    cot_blocks = cotangent.reshape(blocks, TOK_DEV, D).astype(jnp.float32)
    route_blocks = routes.reshape(blocks, TOK_DEV, TOP).astype(jnp.int32)
    gate_blocks = gates.reshape(blocks, TOK_DEV, TOP).astype(jnp.float32)
    positions = jnp.arange(SRC_CAP, dtype=jnp.int32)

    def per_expert(carry, inputs):
        mixed_acc, grad_acc = carry
        w_up, w_down, owner = inputs
        matches = route_blocks == owner
        chosen = jnp.sum(matches.astype(jnp.int32), axis=2)
        weights = jnp.sum(jnp.where(matches, gate_blocks, jnp.float32(0.0)), axis=2)
        ranks = jnp.cumsum(chosen, axis=1) - 1
        placed = (chosen[:, None, :] == 1) & (ranks[:, None, :] == positions[None, :, None])
        placing = placed.astype(jnp.float32)
        slot_gates = jnp.einsum("bct,bt->bc", placing, weights).reshape(-1, 1)
        rows = jnp.einsum("bct,btd->bcd", placing, tok_blocks).reshape(-1, D).astype(jnp.bfloat16)
        pre = jnp.dot(rows, w_up, preferred_element_type=jnp.float32)
        hidden = jax.nn.silu(pre).astype(jnp.bfloat16)
        outputs = jnp.dot(hidden, w_down, preferred_element_type=jnp.float32)
        contrib = (slot_gates * outputs).astype(jnp.bfloat16)
        contrib_blocks = contrib.astype(jnp.float32).reshape(blocks, SRC_CAP, D)
        mixed_acc = mixed_acc + jnp.einsum("bct,bcd->btd", placing, contrib_blocks)
        slot_cot = jnp.einsum("bct,btd->bcd", placing, cot_blocks).reshape(-1, D)
        scaled = (slot_gates * slot_cot).astype(jnp.bfloat16)
        d_hidden = jnp.dot(scaled, w_down.T, preferred_element_type=jnp.float32)
        sig = jax.nn.sigmoid(pre)
        d_pre = (d_hidden * sig * (1.0 + pre * (1.0 - sig))).astype(jnp.bfloat16)
        d_rows = jnp.dot(d_pre, w_up.T, preferred_element_type=jnp.float32).astype(jnp.bfloat16)
        d_blocks = d_rows.astype(jnp.float32).reshape(blocks, SRC_CAP, D)
        grad_acc = grad_acc + jnp.einsum("bct,bcd->btd", placing, d_blocks)
        grad_w = jnp.dot(hidden[:, :FW].T, scaled[:, :DW], preferred_element_type=jnp.float32)
        return (mixed_acc, grad_acc), grad_w

    zeros = jnp.zeros((blocks, TOK_DEV, D), jnp.float32)
    owners = jnp.arange(EXPERTS, dtype=jnp.int32)
    (mixed_sum, grad_sum), grad_down = lax.scan(per_expert, (zeros, zeros), (up_weight, down_weight, owners))
    mixed = mixed_sum.reshape(TOKENS, D).astype(jnp.bfloat16)
    grad_tokens = grad_sum.reshape(TOKENS, D).astype(jnp.bfloat16)
    return mixed, grad_tokens, grad_down
```

```python
import functools

import jax
import jax.numpy as jnp
from jax import lax
from jax.experimental import pallas as pl
from jax.experimental.pallas import tpu as pltpu
from jax.sharding import PartitionSpec as P

F32, BF16 = jnp.float32, jnp.bfloat16
N = 4
CH = 4
MESH = pl.DeviceIdType.MESH


def dot(a, b, ca, cb):
    return lax.dot_general(a, b, (((ca,), (cb,)), ((), ())), preferred_element_type=F32)


def layer_kernel(
    tok, gates, routes, cot, wu, wd,
    mixed, gtok, gdown,
    X, G, SC, Y, R, WU, WD, WG, pre, dh, hid, dpre, GD, S1, R1, S2, R2,
    loc, ag_s, ag_r, rs_s, rs_r, g_s, g_r, p1_s, p1_r, p2_s, p2_r,
):
    T = tok.shape[0]
    W = X.shape[2]
    sh = gdown.shape[0]
    hw = GD.shape[0]
    cols = [slice(c * W, (c + 1) * W) for c in range(CH)]
    z = lax.axis_index("expert")
    p = lax.axis_index("dp")
    core, chip = lax.rem(p, 2), lax.div(p, 2)
    cx, cy = lax.rem(chip, 2), lax.div(chip, 2)
    mates = [chip, (1 - cx) + 2 * cy, cx + 2 * (1 - cy), (1 - cx) + 2 * (1 - cy)]
    other = 2 * chip + 1 - core

    def rows(s):
        return pl.ds(s * T, T)

    def here(fn):
        for k in range(N):
            pl.when(z == k)(functools.partial(fn, k))

    own = pl.ds(pl.multiple_of(z * T, T), T)
    locals_ = {}
    for c in range(CH):
        locals_["x", c] = pltpu.make_async_copy(tok.at[:, pl.ds(c * W, W)], X.at[c, own], loc.at[0, c])
        locals_["g", c] = pltpu.make_async_copy(cot.at[:, pl.ds(c * W, W)], G.at[c, own], loc.at[1, c])
        locals_["u", c] = pltpu.make_async_copy(wu.at[0, pl.ds(c * W, W)], WU.at[c], loc.at[2, c])
        locals_["d", c] = pltpu.make_async_copy(wd.at[0, :, pl.ds(c * W, W)], WD.at[c], loc.at[3, c])
    for name in "xgud":
        for c in range(CH):
            locals_[name, c].start()

    barrier = pltpu.get_barrier_semaphore()
    for d in range(1, N):
        pl.semaphore_signal(barrier, inc=1, device_id={"expert": lax.rem(z + d, N)}, device_id_type=MESH)
    for peer in [other] + [2 * m + core for m in mates[1:]]:
        pl.semaphore_signal(barrier, inc=1, device_id={"dp": peer}, device_id_type=MESH)

    lane = lax.broadcasted_iota(jnp.int32, (T, WG.shape[1]), 1)
    table = jnp.zeros(lane.shape, F32)
    for j in range(routes.shape[1]):
        table += jnp.where(routes[:, j : j + 1] == lane, gates[:, j : j + 1].astype(F32), 0.0)
    WG[own, :] = table.astype(BF16)
    for c in range(CH):
        locals_["x", c].wait()
    pl.semaphore_wait(barrier, 7)

    def ag(ph, c, s, k, step):
        buf = (X, G)[ph].at[c, rows(s)]
        return pltpu.make_async_remote_copy(
            src_ref=buf, dst_ref=buf,
            send_sem=ag_s.at[ph, c, s, (step + 1) // 2], recv_sem=ag_r.at[ph, c, s],
            device_id={"expert": k + step}, device_id_type=MESH,
        )

    def ag_sends(ph, c, k, h):
        if h == 0:
            return [ag(ph, c, k, k, st) for st in (1, -1) if 0 <= k + st < N]
        out = []
        for st in (1, -1):
            if 0 <= k - st * h < N and 0 <= k + st < N:
                out.append(ag(ph, c, k - st * h, k, st))
        return out

    def ag_step(ph, c, h):
        def fn(k):
            for st in (1, -1):
                s = k - st * h
                if 0 <= s < N:
                    ag(ph, c, s, k, st).wait_recv()
                    if 0 <= k + st < N:
                        ag(ph, c, s, k, st).start()

        here(fn)

    def ag_open(ph):
        def fn(k):
            for c in range(CH):
                for cp in ag_sends(ph, c, k, 0):
                    cp.start()

        here(fn)

    def rs(ph, c, s, k):
        step = 1 if s > k else -1
        slot = s + 1 if step == 1 else s
        return pltpu.make_async_remote_copy(
            src_ref=Y.at[ph, c, rows(s)], dst_ref=R.at[ph, c, rows(slot)],
            send_sem=rs_s.at[ph, c, s], recv_sem=rs_r.at[ph, c, slot],
            device_id={"expert": k + step}, device_id_type=MESH,
        )

    def rs_arrived(ph, c, s, k, step):
        slot = s + 1 if step == 1 else s
        pltpu.make_async_remote_copy(
            src_ref=Y.at[ph, c, rows(s)], dst_ref=R.at[ph, c, rows(slot)],
            send_sem=rs_s.at[ph, c, s], recv_sem=rs_r.at[ph, c, slot],
            device_id={"expert": k - step}, device_id_type=MESH,
        ).wait_recv()
        return R[ph, c, rows(slot), :].astype(F32)

    def rs_open(ph, c):
        @pl.when(z == 0)
        def _():
            for s in range(N - 1, 0, -1):
                rs(ph, c, s, 0).start()

        @pl.when(z == N - 1)
        def _():
            for s in range(N - 1):
                rs(ph, c, s, N - 1).start()

    def rs_pass(ph, c):
        def fn(k, step, targets):
            for s in targets:
                got = rs_arrived(ph, c, s, k, step)
                Y[ph, c, rows(s), :] = (Y[ph, c, rows(s), :].astype(F32) + got).astype(BF16)
                rs(ph, c, s, k).start()

        for h in range(1, N - 1):
            k = h
            pl.when(z == k)(functools.partial(fn, k, 1, list(range(N - 1, k, -1))))
            k = N - 1 - h
            pl.when(z == k)(functools.partial(fn, k, -1, list(range(k))))

    def rs_close(ph, c):
        out = (mixed, gtok)[ph]

        def fn(k):
            total = Y[ph, c, rows(k), :].astype(F32)
            if k > 0:
                total += rs_arrived(ph, c, k, k, 1)
            if k < N - 1:
                total += rs_arrived(ph, c, k, k, -1)
            out[:, cols[c]] = total.astype(BF16)

        here(fn)

    def gate(k, s):
        return pltpu.make_async_remote_copy(
            src_ref=WG.at[rows(k)], dst_ref=WG.at[rows(k)],
            send_sem=g_s.at[s], recv_sem=g_r.at[k],
            device_id={"expert": s}, device_id_type=MESH,
        )

    ag_open(0)

    def gate_open(k):
        for s in range(N):
            if s != k:
                gate(k, s).start()

    here(gate_open)

    def up(c):
        locals_["u", c].wait()
        part = dot(X[c], WU[c], 1, 0)
        pre[...] = part if c == 0 else pre[...] + part

    for t in range(CH + 2):
        if t < CH:
            ag_step(0, t, 1)
        if 0 <= t - 1 < CH:
            ag_step(0, t - 1, 2)
        if t == CH:
            for c in range(CH):
                locals_["g", c].wait()
            ag_open(1)
        if 0 <= t - 2 < CH:
            ag_step(0, t - 2, 3)
            up(t - 2)

    def gate_close(k):
        for s in range(N):
            if s != k:
                gate(s, k).wait_recv()

    here(gate_close)
    wide = WG[...].astype(F32)
    gcol = jnp.sum(
        jnp.where(lax.broadcasted_iota(jnp.int32, wide.shape, 1) == z, wide, 0.0), axis=1, keepdims=True
    )
    v = pre[...]
    hid[...] = (v / (1.0 + jnp.exp(-v))).astype(BF16)

    def down(c):
        locals_["d", c].wait()
        Y[0, c] = (gcol * dot(hid[...], WD[c], 1, 0)).astype(BF16)

    def back(c):
        SC[c] = (gcol * G[c].astype(F32)).astype(BF16)
        part = dot(SC[c], WD[c], 1, 1)
        dh[...] = part if c == 0 else dh[...] + part

    def plane1(m):
        return pltpu.make_async_remote_copy(
            src_ref=S1.at[m], dst_ref=R1.at[m], send_sem=p1_s.at[m], recv_sem=p1_r.at[m],
            device_id={"dp": other}, device_id_type=MESH,
        )

    def plane2(d):
        return pltpu.make_async_remote_copy(
            src_ref=S2.at[d - 1], dst_ref=R2.at[d - 1], send_sem=p2_s.at[d - 1], recv_sem=p2_r.at[d - 1],
            device_id={"dp": 2 * mates[d] + core}, device_id_type=MESH,
        )

    def shard(i):
        return pl.ds(pl.multiple_of(i * sh, 16), sh)

    def grads():
        half = hid[:, :hw]
        for c in range(CH // 2):
            GD[:, cols[c]] = dot(half, SC[c], 0, 0)
        for m in range(4):
            S1[m] = GD[shard(2 * m + 1 - core), :].astype(BF16)
            plane1(m).start()

    for c in range(CH):
        down(c)
        rs_open(0, c)
        ag_step(1, c, 1)
        if c >= 1:
            ag_step(1, c - 1, 2)
            rs_pass(0, c - 1)
    ag_step(1, CH - 1, 2)
    rs_pass(0, CH - 1)
    for c in range(CH):
        ag_step(1, c, 3)
        back(c)
        if c == CH // 2 - 1:
            grads()

    sig = 1.0 / (1.0 + jnp.exp(-pre[...]))
    dpre[...] = (dh[...] * sig * (1.0 + pre[...] * (1.0 - sig))).astype(BF16)

    def drows(c):
        Y[1, c] = dot(dpre[...], WU[c], 1, 1).astype(BF16)
        rs_open(1, c)

    for c in range(CH):
        drows(c)
        if c == 0:
            for m in range(4):
                plane1(m).wait_recv()
            for d in range(1, 4):
                S2[d - 1] = (
                    GD[shard(2 * mates[d] + core), :] + R1[mates[d]].astype(F32)
                ).astype(BF16)
                plane2(d).start()
        if c >= 1:
            rs_pass(1, c - 1)
    for c in range(CH):
        rs_close(0, c)
    rs_pass(1, CH - 1)
    total = GD[shard(2 * chip + core), :] + R1[chip].astype(F32)
    for d in range(1, 4):
        plane2(d).wait_recv()
        total += R2[d - 1].astype(F32)
    gdown[...] = total
    for c in range(CH):
        rs_close(1, c)

    def drain(k):
        for ph in range(2):
            for c in range(CH):
                for h in range(N - 1):
                    for cp in ag_sends(ph, c, k, h):
                        cp.wait_send()
                for s in range(N):
                    if s != k:
                        rs(ph, c, s, k).wait_send()
        for s in range(N):
            if s != k:
                gate(k, s).wait_send()

    here(drain)
    for m in range(4):
        plane1(m).wait_send()
    for d in range(1, 4):
        plane2(d).wait_send()


def fused(tokens, gates, routes, cotangent, up_weight, down_weight):
    T, D = tokens.shape
    FF = up_weight.shape[2]
    W = D // CH
    hw, dw = FF // 2, D // 2
    sh = hw // 8
    A = N * T
    dma = pltpu.SemaphoreType.DMA
    anyspace = pl.BlockSpec(memory_space=pl.ANY)
    vmem = pl.BlockSpec(memory_space=pltpu.VMEM)
    mixed, gtok, gdown = pl.pallas_call(
        layer_kernel,
        out_shape=(
            jax.ShapeDtypeStruct((T, D), BF16),
            jax.ShapeDtypeStruct((T, D), BF16),
            jax.ShapeDtypeStruct((sh, dw), F32),
        ),
        in_specs=[anyspace, vmem, vmem, anyspace, anyspace, anyspace],
        out_specs=(vmem, vmem, vmem),
        scratch_shapes=[
            pltpu.VMEM((CH, A, W), BF16),
            pltpu.VMEM((CH, A, W), BF16),
            pltpu.VMEM((CH, A, W), BF16),
            pltpu.VMEM((2, CH, A, W), BF16),
            pltpu.VMEM((2, CH, A + T, W), BF16),
            pltpu.VMEM((CH, W, FF), BF16),
            pltpu.VMEM((CH, FF, W), BF16),
            pltpu.VMEM((A, 128), BF16),
            pltpu.VMEM((A, FF), F32),
            pltpu.VMEM((A, FF), F32),
            pltpu.VMEM((A, FF), BF16),
            pltpu.VMEM((A, FF), BF16),
            pltpu.VMEM((hw, dw), F32),
            pltpu.VMEM((4, sh, dw), BF16),
            pltpu.VMEM((4, sh, dw), BF16),
            pltpu.VMEM((3, sh, dw), BF16),
            pltpu.VMEM((3, sh, dw), BF16),
            dma((4, CH)),
            dma((2, CH, N, 2)),
            dma((2, CH, N)),
            dma((2, CH, N)),
            dma((2, CH, N + 1)),
            dma((N,)),
            dma((N,)),
            dma((4,)),
            dma((4,)),
            dma((3,)),
            dma((3,)),
        ],
        compiler_params=pltpu.CompilerParams(
            collective_id=0, has_side_effects=True, vmem_limit_bytes=44 * 1024 * 1024
        ),
    )(tokens, gates, routes, cotangent, up_weight, down_weight)
    return (mixed, gtok, gdown[None])


def slot_tables(route_blocks, gate_blocks, owners, capacity):
    matches = route_blocks == owners[:, None, None]
    chosen = jnp.sum(matches.astype(jnp.int32), axis=2)
    weights = jnp.sum(jnp.where(matches, gate_blocks.astype(jnp.float32), jnp.float32(0.0)), axis=2)
    ranks = jnp.cumsum(chosen, axis=1) - 1
    positions = jnp.arange(capacity, dtype=jnp.int32)
    placed = (chosen[:, None, :] == 1) & (ranks[:, None, :] == positions[None, :, None])
    placing = placed.astype(jnp.bfloat16)
    slot_gates = jnp.einsum(
        "bct,bt->bc", placing, weights.astype(jnp.bfloat16), preferred_element_type=jnp.float32
    )
    return (placing, slot_gates)


def expert_forward(rows, slot_gates, w_up, w_down):
    pre = jnp.einsum("scd,df->scf", rows, w_up, preferred_element_type=jnp.float32)
    hidden = jax.nn.silu(pre).astype(jnp.bfloat16)
    outputs = jnp.einsum("scf,fd->scd", hidden, w_down, preferred_element_type=jnp.float32)
    contrib = (slot_gates[..., None] * outputs).astype(jnp.bfloat16)
    return (contrib, pre, hidden)


def expert_backward(scaled, pre, w_up, w_down):
    d_hidden = jnp.einsum("scd,fd->scf", scaled, w_down, preferred_element_type=jnp.float32)
    sig = jax.nn.sigmoid(pre)
    d_pre = (d_hidden * sig * (1.0 + pre * (1.0 - sig))).astype(jnp.bfloat16)
    return jnp.einsum("scf,df->scd", d_pre, w_up, preferred_element_type=jnp.float32).astype(
        jnp.bfloat16
    )


def shards(tokens, gates, routes, cotangent, up_weight, down_weight):
    w_up = up_weight[0]
    w_down = down_weight[0]
    tok_dev, width = tokens.shape
    top = routes.shape[1]
    ff_width = w_up.shape[1]
    senders = lax.axis_size("expert")
    experts = senders * up_weight.shape[0]
    capacity = max(2, min(tok_dev, 3 * tok_dev * top // (2 * experts)))
    owners = jnp.arange(senders, dtype=jnp.int32)
    route_blocks = jnp.broadcast_to(routes[None], (senders, tok_dev, top))
    gate_blocks = jnp.broadcast_to(gates[None], (senders, tok_dev, top))
    placing, slot_gates = slot_tables(route_blocks, gate_blocks, owners, capacity)
    rows = jnp.einsum("sct,td->scd", placing, tokens, preferred_element_type=jnp.float32).astype(
        jnp.bfloat16
    )
    arrived = lax.all_to_all(rows, "expert", split_axis=0, concat_axis=0, tiled=True)
    arrived_gates = lax.all_to_all(
        slot_gates.astype(jnp.bfloat16), "expert", split_axis=0, concat_axis=0, tiled=True
    )
    contrib, pre_part, hidden_part = expert_forward(
        arrived, arrived_gates.astype(jnp.float32), w_up, w_down
    )
    returned_part = lax.all_to_all(contrib, "expert", split_axis=0, concat_axis=0, tiled=True)
    mixed = jnp.einsum(
        "sct,scd->td", placing, returned_part, preferred_element_type=jnp.float32
    ).astype(jnp.bfloat16)
    slot_cot = jnp.einsum(
        "sct,td->scd", placing, cotangent, preferred_element_type=jnp.float32
    ).astype(jnp.bfloat16)
    outgoing = (slot_gates[..., None] * slot_cot.astype(jnp.float32)).astype(jnp.bfloat16)
    scaled = lax.all_to_all(outgoing, "expert", split_axis=0, concat_axis=0, tiled=True)
    d_rows = expert_backward(scaled, pre_part, w_up, w_down)
    came_back = lax.all_to_all(d_rows, "expert", split_axis=0, concat_axis=0, tiled=True)
    grad_tokens = jnp.einsum(
        "sct,scd->td", placing, came_back, preferred_element_type=jnp.float32
    ).astype(jnp.bfloat16)
    window_ff = ff_width // 2
    window_d = width // 2
    flat_hidden = hidden_part.reshape(-1, ff_width)[:, :window_ff]
    flat_scaled = scaled.reshape(-1, width)[:, :window_d]
    grad_down = lax.psum_scatter(
        lax.dot_general(
            flat_hidden, flat_scaled, (((0,), (0,)), ((), ())), preferred_element_type=jnp.float32
        ),
        "dp",
        scatter_dimension=0,
        tiled=True,
    )
    return (mixed, grad_tokens, grad_down[None])


def solution(mesh):
    chain = mesh.shape["dp"] == 8 and mesh.shape["expert"] == N
    return jax.shard_map(
        fused if chain else shards,
        mesh=mesh,
        in_specs=(
            P(("dp", "expert"), None),
            P(("dp", "expert"), None),
            P(("dp", "expert"), None),
            P(("dp", "expert"), None),
            P("expert", None, None),
            P("expert", None, None),
        ),
        out_specs=(P(("dp", "expert"), None), P(("dp", "expert"), None), P("expert", "dp", None)),
        check_vma=False,
    )
```

```python
import functools

import jax
import jax.numpy as jnp
from jax import lax
from jax.experimental import pallas as pl
from jax.experimental.pallas import tpu as pltpu
from jax.sharding import PartitionSpec as P

F32, BF16 = jnp.float32, jnp.bfloat16
N = 4
CH = 4
WINDOW = 4
MESH = pl.DeviceIdType.MESH


def dot(a, b, ca, cb):
    return lax.dot_general(a, b, (((ca,), (cb,)), ((), ())), preferred_element_type=F32)


def layer_kernel(
    tok, gates, routes, cot, wu, wd,
    mixed, gtok, gdown,
    X, G, SC, Y, R, WU, WD, WG, pre, dh, hid, dpre, GD, S1, R1, S2, R2,
    loc, ag_s, ag_r, rs_s, rs_r, g_s, g_r, p1_s, p1_r, p2_s, p2_r,
):
    T = tok.shape[0]
    W = X.shape[2]
    sh = gdown.shape[0]
    hw = GD.shape[0]
    cols = [slice(c * W, (c + 1) * W) for c in range(CH)]
    z = lax.axis_index("expert")
    p = lax.axis_index("dp")
    core, chip = lax.rem(p, 2), lax.div(p, 2)
    cx, cy = lax.rem(chip, 2), lax.div(chip, 2)
    mates = [chip, (1 - cx) + 2 * cy, cx + 2 * (1 - cy), (1 - cx) + 2 * (1 - cy)]
    other = 2 * chip + 1 - core

    def rows(s):
        return pl.ds(s * T, T)

    def here(fn):
        for k in range(N):
            pl.when(z == k)(functools.partial(fn, k))

    own = pl.ds(pl.multiple_of(z * T, T), T)
    locals_ = {}
    for c in range(CH):
        locals_["x", c] = pltpu.make_async_copy(tok.at[:, pl.ds(c * W, W)], X.at[c, own], loc.at[0, c])
        locals_["g", c] = pltpu.make_async_copy(cot.at[:, pl.ds(c * W, W)], G.at[c, own], loc.at[1, c])
        locals_["u", c] = pltpu.make_async_copy(wu.at[0, pl.ds(c * W, W)], WU.at[c], loc.at[2, c])
        locals_["d", c] = pltpu.make_async_copy(wd.at[0, :, pl.ds(c * W, W)], WD.at[c], loc.at[3, c])
    for name in "xgud":
        for c in range(CH):
            locals_[name, c].start()

    barrier = pltpu.get_barrier_semaphore()
    for d in range(1, N):
        pl.semaphore_signal(barrier, inc=1, device_id={"expert": lax.rem(z + d, N)}, device_id_type=MESH)
    for peer in [other] + [2 * m + core for m in mates[1:]]:
        pl.semaphore_signal(barrier, inc=1, device_id={"dp": peer}, device_id_type=MESH)

    expert = lax.broadcasted_iota(jnp.int32, (WG.shape[1], T), 0)
    table = jnp.zeros(expert.shape, F32)
    for j in range(routes.shape[0]):
        table += jnp.where(routes[j : j + 1, :] == expert, gates[j : j + 1, :].astype(F32), 0.0)
    eye = lax.broadcasted_iota(jnp.int32, (T, T), 0) == lax.broadcasted_iota(jnp.int32, (T, T), 1)
    WG[own, :] = dot(eye.astype(F32).astype(BF16), table.astype(BF16), 1, 1).astype(BF16)
    for c in range(CH):
        locals_["x", c].wait()
    pl.semaphore_wait(barrier, 7)

    def ag(ph, c, s, k, step):
        buf = (X, G)[ph].at[c, rows(s)]
        return pltpu.make_async_remote_copy(
            src_ref=buf, dst_ref=buf,
            send_sem=ag_s.at[ph, c, s, (step + 1) // 2], recv_sem=ag_r.at[ph, c, s],
            device_id={"expert": k + step}, device_id_type=MESH,
        )

    def ag_sends(ph, c, k, h):
        if h == 0:
            return [ag(ph, c, k, k, st) for st in (1, -1) if 0 <= k + st < N]
        out = []
        for st in (1, -1):
            if 0 <= k - st * h < N and 0 <= k + st < N:
                out.append(ag(ph, c, k - st * h, k, st))
        return out

    def ag_step(ph, c, h):
        def fn(k):
            for st in (1, -1):
                s = k - st * h
                if 0 <= s < N:
                    ag(ph, c, s, k, st).wait_recv()
                    if 0 <= k + st < N:
                        ag(ph, c, s, k, st).start()

        here(fn)

    def ag_open(ph):
        def fn(k):
            for c in range(CH):
                for cp in ag_sends(ph, c, k, 0):
                    cp.start()

        here(fn)

    def rs(ph, c, s, k):
        step = 1 if s > k else -1
        slot = s + 1 if step == 1 else s
        return pltpu.make_async_remote_copy(
            src_ref=Y.at[ph, c, rows(s)], dst_ref=R.at[ph, c, rows(slot)],
            send_sem=rs_s.at[ph, c, s], recv_sem=rs_r.at[ph, c, slot],
            device_id={"expert": k + step}, device_id_type=MESH,
        )

    def rs_arrived(ph, c, s, k, step):
        slot = s + 1 if step == 1 else s
        pltpu.make_async_remote_copy(
            src_ref=Y.at[ph, c, rows(s)], dst_ref=R.at[ph, c, rows(slot)],
            send_sem=rs_s.at[ph, c, s], recv_sem=rs_r.at[ph, c, slot],
            device_id={"expert": k - step}, device_id_type=MESH,
        ).wait_recv()
        return R[ph, c, rows(slot), :].astype(F32)

    def rs_open(ph):
        def fn(k, targets):
            sent = [rs(ph, c, s, k) for s in targets for c in range(CH)]
            for i, cp in enumerate(sent):
                if i >= WINDOW:
                    sent[i - WINDOW].wait_send()
                cp.start()

        pl.when(z == 0)(functools.partial(fn, 0, list(range(N - 1, 0, -1))))
        pl.when(z == N - 1)(functools.partial(fn, N - 1, list(range(N - 1))))

    def rs_left(k):
        targets = list(range(N - 1, 0, -1)) if k == 0 else [s for s in range(N) if s != k]
        every = [(s, c) for s in targets for c in range(CH)]
        return every[-WINDOW:] if k in (0, N - 1) else every

    def rs_pass(ph):
        def add(c, s, k, step):
            got = rs_arrived(ph, c, s, k, step)
            Y[ph, c, rows(s), :] = (Y[ph, c, rows(s), :].astype(F32) + got).astype(BF16)
            rs(ph, c, s, k).start()

        def fn(k, step, far, near, back_to):
            for c in range(CH):
                add(c, far, k, step)
            for c in range(CH):
                add(c, near, k, step)
                add(c, back_to, k, -step)

        pl.when(z == 1)(functools.partial(fn, 1, 1, 3, 2, 0))
        pl.when(z == 2)(functools.partial(fn, 2, -1, 0, 1, 3))

    def rs_close(ph, c):
        out = (mixed, gtok)[ph]

        def fn(k):
            total = Y[ph, c, rows(k), :].astype(F32)
            if k > 0:
                total += rs_arrived(ph, c, k, k, 1)
            if k < N - 1:
                total += rs_arrived(ph, c, k, k, -1)
            out[:, cols[c]] = total.astype(BF16)

        here(fn)

    def gate(k, s):
        return pltpu.make_async_remote_copy(
            src_ref=WG.at[rows(k)], dst_ref=WG.at[rows(k)],
            send_sem=g_s.at[s], recv_sem=g_r.at[k],
            device_id={"expert": s}, device_id_type=MESH,
        )

    ag_open(0)

    def gate_open(k):
        for s in range(N):
            if s != k:
                gate(k, s).start()

    here(gate_open)

    def up(c):
        locals_["u", c].wait()
        part = dot(X[c], WU[c], 1, 0)
        pre[...] = part if c == 0 else pre[...] + part

    for t in range(CH + 2):
        if t < CH:
            ag_step(0, t, 1)
        if 0 <= t - 1 < CH:
            ag_step(0, t - 1, 2)
        if t == CH:
            for c in range(CH):
                locals_["g", c].wait()
            ag_open(1)
        if 0 <= t - 2 < CH:
            ag_step(0, t - 2, 3)
            up(t - 2)

    def gate_close(k):
        for s in range(N):
            if s != k:
                gate(s, k).wait_recv()

    here(gate_close)
    wide = WG[...].astype(F32)
    gcol = jnp.sum(
        jnp.where(lax.broadcasted_iota(jnp.int32, wide.shape, 1) == z, wide, 0.0), axis=1, keepdims=True
    )
    v = pre[...]
    hid[...] = (v / (1.0 + jnp.exp(-v))).astype(BF16)

    def down(c):
        locals_["d", c].wait()
        Y[0, c] = (gcol * dot(hid[...], WD[c], 1, 0)).astype(BF16)

    def back(c):
        SC[c] = (gcol * G[c].astype(F32)).astype(BF16)
        part = dot(SC[c], WD[c], 1, 1)
        dh[...] = part if c == 0 else dh[...] + part

    def plane1(m):
        return pltpu.make_async_remote_copy(
            src_ref=S1.at[m], dst_ref=R1.at[m], send_sem=p1_s.at[m], recv_sem=p1_r.at[m],
            device_id={"dp": other}, device_id_type=MESH,
        )

    def plane2(d):
        return pltpu.make_async_remote_copy(
            src_ref=S2.at[d - 1], dst_ref=R2.at[d - 1], send_sem=p2_s.at[d - 1], recv_sem=p2_r.at[d - 1],
            device_id={"dp": 2 * mates[d] + core}, device_id_type=MESH,
        )

    def shard(i):
        return pl.ds(pl.multiple_of(i * sh, 16), sh)

    def grads():
        half = hid[:, :hw]
        for c in range(CH // 2):
            GD[:, cols[c]] = dot(half, SC[c], 0, 0)
        for m in range(4):
            S1[m] = GD[shard(2 * m + 1 - core), :].astype(BF16)
            plane1(m).start()

    for c in range(CH):
        down(c)
    rs_open(0)
    for c in range(CH):
        ag_step(1, c, 1)
    for c in range(CH):
        ag_step(1, c, 2)
    for c in range(CH):
        ag_step(1, c, 3)
        back(c)
        if c == CH // 2 - 1:
            grads()

    sig = 1.0 / (1.0 + jnp.exp(-pre[...]))
    dpre[...] = (dh[...] * sig * (1.0 + pre[...] * (1.0 - sig))).astype(BF16)
    for c in range(CH):
        Y[1, c] = dot(dpre[...], WU[c], 1, 1).astype(BF16)
    for m in range(4):
        plane1(m).wait_recv()
    for d in range(1, 4):
        S2[d - 1] = (GD[shard(2 * mates[d] + core), :] + R1[mates[d]].astype(F32)).astype(BF16)
        plane2(d).start()
    rs_open(1)
    rs_pass(0)
    rs_pass(1)
    for c in range(CH):
        rs_close(0, c)
    total = GD[shard(2 * chip + core), :] + R1[chip].astype(F32)
    for d in range(1, 4):
        plane2(d).wait_recv()
        total += R2[d - 1].astype(F32)
    gdown[...] = total
    for c in range(CH):
        rs_close(1, c)

    def drain(k):
        for ph in range(2):
            for c in range(CH):
                for h in range(N - 1):
                    for cp in ag_sends(ph, c, k, h):
                        cp.wait_send()
            for s, c in rs_left(k):
                rs(ph, c, s, k).wait_send()
        for s in range(N):
            if s != k:
                gate(k, s).wait_send()

    here(drain)
    for m in range(4):
        plane1(m).wait_send()
    for d in range(1, 4):
        plane2(d).wait_send()


def fused(tokens, gates, routes, cotangent, up_weight, down_weight):
    T, D = tokens.shape
    FF = up_weight.shape[2]
    W = D // CH
    hw, dw = FF // 2, D // 2
    sh = hw // 8
    A = N * T
    dma = pltpu.SemaphoreType.DMA
    anyspace = pl.BlockSpec(memory_space=pl.ANY)
    vmem = pl.BlockSpec(memory_space=pltpu.VMEM)
    mixed, gtok, gdown = pl.pallas_call(
        layer_kernel,
        out_shape=(
            jax.ShapeDtypeStruct((T, D), BF16),
            jax.ShapeDtypeStruct((T, D), BF16),
            jax.ShapeDtypeStruct((sh, dw), F32),
        ),
        in_specs=[anyspace, vmem, vmem, anyspace, anyspace, anyspace],
        out_specs=(vmem, vmem, vmem),
        scratch_shapes=[
            pltpu.VMEM((CH, A, W), BF16),
            pltpu.VMEM((CH, A, W), BF16),
            pltpu.VMEM((CH, A, W), BF16),
            pltpu.VMEM((2, CH, A, W), BF16),
            pltpu.VMEM((2, CH, A + T, W), BF16),
            pltpu.VMEM((CH, W, FF), BF16),
            pltpu.VMEM((CH, FF, W), BF16),
            pltpu.VMEM((A, 128), BF16),
            pltpu.VMEM((A, FF), F32),
            pltpu.VMEM((A, FF), F32),
            pltpu.VMEM((A, FF), BF16),
            pltpu.VMEM((A, FF), BF16),
            pltpu.VMEM((hw, dw), F32),
            pltpu.VMEM((4, sh, dw), BF16),
            pltpu.VMEM((4, sh, dw), BF16),
            pltpu.VMEM((3, sh, dw), BF16),
            pltpu.VMEM((3, sh, dw), BF16),
            dma((4, CH)),
            dma((2, CH, N, 2)),
            dma((2, CH, N)),
            dma((2, CH, N)),
            dma((2, CH, N + 1)),
            dma((N,)),
            dma((N,)),
            dma((4,)),
            dma((4,)),
            dma((3,)),
            dma((3,)),
        ],
        compiler_params=pltpu.CompilerParams(
            collective_id=0, has_side_effects=True, vmem_limit_bytes=60 * 1024 * 1024
        ),
    )(tokens, gates.T, routes.T, cotangent, up_weight, down_weight)
    return (mixed, gtok, gdown[None])


def slot_tables(route_blocks, gate_blocks, owners, capacity):
    matches = route_blocks == owners[:, None, None]
    chosen = jnp.sum(matches.astype(jnp.int32), axis=2)
    weights = jnp.sum(jnp.where(matches, gate_blocks.astype(jnp.float32), jnp.float32(0.0)), axis=2)
    ranks = jnp.cumsum(chosen, axis=1) - 1
    positions = jnp.arange(capacity, dtype=jnp.int32)
    placed = (chosen[:, None, :] == 1) & (ranks[:, None, :] == positions[None, :, None])
    placing = placed.astype(jnp.bfloat16)
    slot_gates = jnp.einsum(
        "bct,bt->bc", placing, weights.astype(jnp.bfloat16), preferred_element_type=jnp.float32
    )
    return (placing, slot_gates)


def expert_forward(rows, slot_gates, w_up, w_down):
    pre = jnp.einsum("scd,df->scf", rows, w_up, preferred_element_type=jnp.float32)
    hidden = jax.nn.silu(pre).astype(jnp.bfloat16)
    outputs = jnp.einsum("scf,fd->scd", hidden, w_down, preferred_element_type=jnp.float32)
    contrib = (slot_gates[..., None] * outputs).astype(jnp.bfloat16)
    return (contrib, pre, hidden)


def expert_backward(scaled, pre, w_up, w_down):
    d_hidden = jnp.einsum("scd,fd->scf", scaled, w_down, preferred_element_type=jnp.float32)
    sig = jax.nn.sigmoid(pre)
    d_pre = (d_hidden * sig * (1.0 + pre * (1.0 - sig))).astype(jnp.bfloat16)
    return jnp.einsum("scf,df->scd", d_pre, w_up, preferred_element_type=jnp.float32).astype(
        jnp.bfloat16
    )


def shards(tokens, gates, routes, cotangent, up_weight, down_weight):
    w_up = up_weight[0]
    w_down = down_weight[0]
    tok_dev, width = tokens.shape
    top = routes.shape[1]
    ff_width = w_up.shape[1]
    senders = lax.axis_size("expert")
    experts = senders * up_weight.shape[0]
    capacity = max(2, min(tok_dev, 3 * tok_dev * top // (2 * experts)))
    owners = jnp.arange(senders, dtype=jnp.int32)
    route_blocks = jnp.broadcast_to(routes[None], (senders, tok_dev, top))
    gate_blocks = jnp.broadcast_to(gates[None], (senders, tok_dev, top))
    placing, slot_gates = slot_tables(route_blocks, gate_blocks, owners, capacity)
    rows = jnp.einsum("sct,td->scd", placing, tokens, preferred_element_type=jnp.float32).astype(
        jnp.bfloat16
    )
    arrived = lax.all_to_all(rows, "expert", split_axis=0, concat_axis=0, tiled=True)
    arrived_gates = lax.all_to_all(
        slot_gates.astype(jnp.bfloat16), "expert", split_axis=0, concat_axis=0, tiled=True
    )
    contrib, pre_part, hidden_part = expert_forward(
        arrived, arrived_gates.astype(jnp.float32), w_up, w_down
    )
    returned_part = lax.all_to_all(contrib, "expert", split_axis=0, concat_axis=0, tiled=True)
    mixed = jnp.einsum(
        "sct,scd->td", placing, returned_part, preferred_element_type=jnp.float32
    ).astype(jnp.bfloat16)
    slot_cot = jnp.einsum(
        "sct,td->scd", placing, cotangent, preferred_element_type=jnp.float32
    ).astype(jnp.bfloat16)
    outgoing = (slot_gates[..., None] * slot_cot.astype(jnp.float32)).astype(jnp.bfloat16)
    scaled = lax.all_to_all(outgoing, "expert", split_axis=0, concat_axis=0, tiled=True)
    d_rows = expert_backward(scaled, pre_part, w_up, w_down)
    came_back = lax.all_to_all(d_rows, "expert", split_axis=0, concat_axis=0, tiled=True)
    grad_tokens = jnp.einsum(
        "sct,scd->td", placing, came_back, preferred_element_type=jnp.float32
    ).astype(jnp.bfloat16)
    window_ff = ff_width // 2
    window_d = width // 2
    flat_hidden = hidden_part.reshape(-1, ff_width)[:, :window_ff]
    flat_scaled = scaled.reshape(-1, width)[:, :window_d]
    grad_down = lax.psum_scatter(
        lax.dot_general(
            flat_hidden, flat_scaled, (((0,), (0,)), ((), ())), preferred_element_type=jnp.float32
        ),
        "dp",
        scatter_dimension=0,
        tiled=True,
    )
    return (mixed, grad_tokens, grad_down[None])


def solution(mesh):
    chain = mesh.shape["dp"] == 8 and mesh.shape["expert"] == N
    return jax.shard_map(
        fused if chain else shards,
        mesh=mesh,
        in_specs=(
            P(("dp", "expert"), None),
            P(("dp", "expert"), None),
            P(("dp", "expert"), None),
            P(("dp", "expert"), None),
            P("expert", None, None),
            P("expert", None, None),
        ),
        out_specs=(P(("dp", "expert"), None), P(("dp", "expert"), None), P("expert", "dp", None)),
        check_vma=False,
    )
```

```python
import functools

import jax
import jax.numpy as jnp
from jax import lax
from jax.experimental import pallas as pl
from jax.experimental.pallas import tpu as pltpu
from jax.sharding import PartitionSpec as P

F32, BF16 = jnp.float32, jnp.bfloat16
N = 4
CH = 4
MESH = pl.DeviceIdType.MESH


def dot(a, b, ca, cb):
    return lax.dot_general(a, b, (((ca,), (cb,)), ((), ())), preferred_element_type=F32)


def layer_kernel(
    tok, gates, routes, cot, wu, wd,
    mixed, gtok, gdown,
    X, G, SC, Y, R, WU, WD, WG, pre, hid, GD, S1, R1, S2, R2,
    loc, ag_s, ag_r, rs_s, rs_r, g_s, g_r, p1_s, p1_r, p2_s, p2_r,
):
    T = tok.shape[0]
    W = X.shape[2]
    sh = gdown.shape[0]
    hw = GD.shape[0]
    cols = [slice(c * W, (c + 1) * W) for c in range(CH)]
    z = lax.axis_index("expert")
    p = lax.axis_index("dp")
    core, chip = lax.rem(p, 2), lax.div(p, 2)
    cx, cy = lax.rem(chip, 2), lax.div(chip, 2)
    mates = [chip, (1 - cx) + 2 * cy, cx + 2 * (1 - cy), (1 - cx) + 2 * (1 - cy)]
    other = 2 * chip + 1 - core

    def rows(s):
        return pl.ds(s * T, T)

    def here(fn):
        for k in range(N):
            pl.when(z == k)(functools.partial(fn, k))

    own = pl.ds(pl.multiple_of(z * T, T), T)
    locals_ = {}
    for c in range(CH):
        locals_["x", c] = pltpu.make_async_copy(tok.at[:, pl.ds(c * W, W)], X.at[c, own], loc.at[0, c])
        locals_["g", c] = pltpu.make_async_copy(cot.at[:, pl.ds(c * W, W)], G.at[c, own], loc.at[1, c])
        locals_["u", c] = pltpu.make_async_copy(wu.at[0, pl.ds(c * W, W)], WU.at[c], loc.at[2, c])
        locals_["d", c] = pltpu.make_async_copy(wd.at[0, :, pl.ds(c * W, W)], WD.at[c], loc.at[3, c])
    for name in "xgud":
        for c in range(CH):
            locals_[name, c].start()

    barrier = pltpu.get_barrier_semaphore()
    for d in range(1, N):
        pl.semaphore_signal(barrier, inc=1, device_id={"expert": lax.rem(z + d, N)}, device_id_type=MESH)
    for peer in [other] + [2 * m + core for m in mates[1:]]:
        pl.semaphore_signal(barrier, inc=1, device_id={"dp": peer}, device_id_type=MESH)

    expert = lax.broadcasted_iota(jnp.int32, (WG.shape[1], T), 0)
    table = jnp.zeros(expert.shape, F32)
    for j in range(routes.shape[0]):
        table += jnp.where(routes[j : j + 1, :] == expert, gates[j : j + 1, :].astype(F32), 0.0)
    eye = lax.broadcasted_iota(jnp.int32, (T, T), 0) == lax.broadcasted_iota(jnp.int32, (T, T), 1)
    WG[own, :] = dot(eye.astype(F32).astype(BF16), table.astype(BF16), 1, 1).astype(BF16)
    for c in range(CH):
        locals_["x", c].wait()
    pl.semaphore_wait(barrier, 7)

    def ag(ph, c, s, k, step):
        buf = (X, G)[ph].at[c, rows(s)]
        return pltpu.make_async_remote_copy(
            src_ref=buf, dst_ref=buf,
            send_sem=ag_s.at[ph, c, s, (step + 1) // 2], recv_sem=ag_r.at[ph, c, s],
            device_id={"expert": k + step}, device_id_type=MESH,
        )

    def ag_sends(ph, c, k, h):
        if h == 0:
            return [ag(ph, c, k, k, st) for st in (1, -1) if 0 <= k + st < N]
        out = []
        for st in (1, -1):
            if 0 <= k - st * h < N and 0 <= k + st < N:
                out.append(ag(ph, c, k - st * h, k, st))
        return out

    def ag_step(ph, c, h):
        def fn(k):
            for st in (1, -1):
                s = k - st * h
                if 0 <= s < N:
                    ag(ph, c, s, k, st).wait_recv()
                    if 0 <= k + st < N:
                        ag(ph, c, s, k, st).start()

        here(fn)

    def ag_open(ph):
        def fn(k):
            for c in range(CH):
                for cp in ag_sends(ph, c, k, 0):
                    cp.start()

        here(fn)

    def rs(ph, c, s, k):
        step = 1 if s > k else -1
        slot = s + 1 if step == 1 else s
        return pltpu.make_async_remote_copy(
            src_ref=Y.at[ph, c, rows(s)], dst_ref=R.at[ph, c, rows(slot)],
            send_sem=rs_s.at[ph, c, s], recv_sem=rs_r.at[ph, c, slot],
            device_id={"expert": k + step}, device_id_type=MESH,
        )

    def rs_arrived(ph, c, s, k, step):
        slot = s + 1 if step == 1 else s
        pltpu.make_async_remote_copy(
            src_ref=Y.at[ph, c, rows(s)], dst_ref=R.at[ph, c, rows(slot)],
            send_sem=rs_s.at[ph, c, s], recv_sem=rs_r.at[ph, c, slot],
            device_id={"expert": k - step}, device_id_type=MESH,
        ).wait_recv()
        return R[ph, c, rows(slot), :].astype(F32)

    def rs_open(ph, c, i):
        pl.when(z == 0)(lambda: rs(ph, c, i, 0).start())
        pl.when(z == N - 1)(lambda: rs(ph, c, N - 1 - i, N - 1).start())

    def rs_pass(ph):
        def fn(k, order):
            for s, step in order:
                for c in range(CH):
                    got = rs_arrived(ph, c, s, k, step)
                    Y[ph, c, rows(s), :] = (Y[ph, c, rows(s), :].astype(F32) + got).astype(BF16)
                    rs(ph, c, s, k).start()

        pl.when(z == 1)(functools.partial(fn, 1, [(2, 1), (3, 1), (0, -1)]))
        pl.when(z == 2)(functools.partial(fn, 2, [(1, -1), (0, -1), (3, 1)]))

    def rs_close(ph, c):
        out = (mixed, gtok)[ph]

        def fn(k):
            total = Y[ph, c, rows(k), :].astype(F32)
            if k > 0:
                total += rs_arrived(ph, c, k, k, 1)
            if k < N - 1:
                total += rs_arrived(ph, c, k, k, -1)
            out[:, cols[c]] = total.astype(BF16)

        here(fn)

    def gate(k, s):
        return pltpu.make_async_remote_copy(
            src_ref=WG.at[rows(k)], dst_ref=WG.at[rows(k)],
            send_sem=g_s.at[s], recv_sem=g_r.at[k],
            device_id={"expert": s}, device_id_type=MESH,
        )

    ag_open(0)

    def gate_open(k):
        for s in range(N):
            if s != k:
                gate(k, s).start()

    here(gate_open)

    def gate_close(k):
        for s in range(N):
            if s != k:
                gate(s, k).wait_recv()

    low = z < N // 2
    inner = (z == 1) | (z == 2)
    toward = jnp.where(low, 1, -1)
    order = [
        z,
        jnp.where(inner, z - toward, z + toward),
        jnp.where(inner, z + toward, z + 2 * toward),
        jnp.where(inner, z + 2 * toward, z + 3 * toward),
    ]
    spans = [pl.ds(pl.multiple_of(s * T, T), T) for s in order]

    def gate_column(at):
        wide = WG[at, :].astype(F32)
        mine = lax.broadcasted_iota(jnp.int32, wide.shape, 1) == z
        return jnp.sum(jnp.where(mine, wide, 0.0), axis=1, keepdims=True)

    def forward(i):
        at = spans[i]
        v = None
        for c in range(CH):
            if i == 0:
                locals_["u", c].wait()
            part = dot(X[c, at, :], WU[c], 1, 0)
            v = part if c == 0 else v + part
        pre[at, :] = v
        h = (v / (1.0 + jnp.exp(-v))).astype(BF16)
        hid[at, :] = h
        gcol = gate_column(at)
        for c in range(CH):
            if i == 0:
                locals_["d", c].wait()
            Y[0, c, at, :] = (gcol * dot(h, WD[c], 1, 0)).astype(BF16)
            if i:
                rs_open(0, c, i)

    def backward(i):
        at = spans[i]
        gcol = gate_column(at)
        d = None
        for c in range(CH):
            scaled = (gcol * G[c, at, :].astype(F32)).astype(BF16)
            SC[c, at, :] = scaled
            part = dot(scaled, WD[c], 1, 1)
            d = part if c == 0 else d + part
        v = pre[at, :]
        sig = 1.0 / (1.0 + jnp.exp(-v))
        dp = (d * sig * (1.0 + v * (1.0 - sig))).astype(BF16)
        for c in range(CH):
            Y[1, c, at, :] = dot(dp, WU[c], 1, 1).astype(BF16)
            if i:
                rs_open(1, c, i)

    def plane1(m):
        return pltpu.make_async_remote_copy(
            src_ref=S1.at[m], dst_ref=R1.at[m], send_sem=p1_s.at[m], recv_sem=p1_r.at[m],
            device_id={"dp": other}, device_id_type=MESH,
        )

    def plane2(d):
        return pltpu.make_async_remote_copy(
            src_ref=S2.at[d - 1], dst_ref=R2.at[d - 1], send_sem=p2_s.at[d - 1], recv_sem=p2_r.at[d - 1],
            device_id={"dp": 2 * mates[d] + core}, device_id_type=MESH,
        )

    def shard(i):
        return pl.ds(pl.multiple_of(i * sh, 16), sh)

    def grads():
        half = hid[:, :hw]
        for c in range(CH // 2):
            GD[:, cols[c]] = dot(half, SC[c], 0, 0)
        for m in range(4):
            S1[m] = GD[shard(2 * m + 1 - core), :].astype(BF16)
            plane1(m).start()

    forward(0)
    here(gate_close)
    for c in range(CH):
        ag_step(0, c, 1)
    forward(1)
    for c in range(CH):
        ag_step(0, c, 2)
    for c in range(CH):
        locals_["g", c].wait()
    ag_open(1)
    forward(2)
    for c in range(CH):
        ag_step(0, c, 3)
    forward(3)
    backward(0)
    for c in range(CH):
        ag_step(1, c, 1)
    backward(1)
    for c in range(CH):
        ag_step(1, c, 2)
    backward(2)
    for c in range(CH):
        ag_step(1, c, 3)
    backward(3)
    grads()
    rs_pass(0)
    for m in range(4):
        plane1(m).wait_recv()
    for d in range(1, 4):
        S2[d - 1] = (GD[shard(2 * mates[d] + core), :] + R1[mates[d]].astype(F32)).astype(BF16)
        plane2(d).start()
    rs_pass(1)
    for c in range(CH):
        rs_close(0, c)
    total = GD[shard(2 * chip + core), :] + R1[chip].astype(F32)
    for d in range(1, 4):
        plane2(d).wait_recv()
        total += R2[d - 1].astype(F32)
    gdown[...] = total
    for c in range(CH):
        rs_close(1, c)

    def drain(k):
        for ph in range(2):
            for c in range(CH):
                for h in range(N - 1):
                    for cp in ag_sends(ph, c, k, h):
                        cp.wait_send()
                for s in range(N):
                    if s != k:
                        rs(ph, c, s, k).wait_send()
        for s in range(N):
            if s != k:
                gate(k, s).wait_send()

    here(drain)
    for m in range(4):
        plane1(m).wait_send()
    for d in range(1, 4):
        plane2(d).wait_send()


def fused(tokens, gates, routes, cotangent, up_weight, down_weight):
    T, D = tokens.shape
    FF = up_weight.shape[2]
    W = D // CH
    hw, dw = FF // 2, D // 2
    sh = hw // 8
    A = N * T
    dma = pltpu.SemaphoreType.DMA
    anyspace = pl.BlockSpec(memory_space=pl.ANY)
    vmem = pl.BlockSpec(memory_space=pltpu.VMEM)
    mixed, gtok, gdown = pl.pallas_call(
        layer_kernel,
        out_shape=(
            jax.ShapeDtypeStruct((T, D), BF16),
            jax.ShapeDtypeStruct((T, D), BF16),
            jax.ShapeDtypeStruct((sh, dw), F32),
        ),
        in_specs=[anyspace, vmem, vmem, anyspace, anyspace, anyspace],
        out_specs=(vmem, vmem, vmem),
        scratch_shapes=[
            pltpu.VMEM((CH, A, W), BF16),
            pltpu.VMEM((CH, A, W), BF16),
            pltpu.VMEM((CH, A, W), BF16),
            pltpu.VMEM((2, CH, A, W), BF16),
            pltpu.VMEM((2, CH, A + T, W), BF16),
            pltpu.VMEM((CH, W, FF), BF16),
            pltpu.VMEM((CH, FF, W), BF16),
            pltpu.VMEM((A, 128), BF16),
            pltpu.VMEM((A, FF), F32),
            pltpu.VMEM((A, FF), BF16),
            pltpu.VMEM((hw, dw), F32),
            pltpu.VMEM((4, sh, dw), BF16),
            pltpu.VMEM((4, sh, dw), BF16),
            pltpu.VMEM((3, sh, dw), BF16),
            pltpu.VMEM((3, sh, dw), BF16),
            dma((4, CH)),
            dma((2, CH, N, 2)),
            dma((2, CH, N)),
            dma((2, CH, N)),
            dma((2, CH, N + 1)),
            dma((N,)),
            dma((N,)),
            dma((4,)),
            dma((4,)),
            dma((3,)),
            dma((3,)),
        ],
        compiler_params=pltpu.CompilerParams(
            collective_id=0, has_side_effects=True, vmem_limit_bytes=60 * 1024 * 1024
        ),
    )(tokens, gates.T, routes.T, cotangent, up_weight, down_weight)
    return (mixed, gtok, gdown[None])


def slot_tables(route_blocks, gate_blocks, owners, capacity):
    matches = route_blocks == owners[:, None, None]
    chosen = jnp.sum(matches.astype(jnp.int32), axis=2)
    weights = jnp.sum(jnp.where(matches, gate_blocks.astype(jnp.float32), jnp.float32(0.0)), axis=2)
    ranks = jnp.cumsum(chosen, axis=1) - 1
    positions = jnp.arange(capacity, dtype=jnp.int32)
    placed = (chosen[:, None, :] == 1) & (ranks[:, None, :] == positions[None, :, None])
    placing = placed.astype(jnp.bfloat16)
    slot_gates = jnp.einsum(
        "bct,bt->bc", placing, weights.astype(jnp.bfloat16), preferred_element_type=jnp.float32
    )
    return (placing, slot_gates)


def expert_forward(rows, slot_gates, w_up, w_down):
    pre = jnp.einsum("scd,df->scf", rows, w_up, preferred_element_type=jnp.float32)
    hidden = jax.nn.silu(pre).astype(jnp.bfloat16)
    outputs = jnp.einsum("scf,fd->scd", hidden, w_down, preferred_element_type=jnp.float32)
    contrib = (slot_gates[..., None] * outputs).astype(jnp.bfloat16)
    return (contrib, pre, hidden)


def expert_backward(scaled, pre, w_up, w_down):
    d_hidden = jnp.einsum("scd,fd->scf", scaled, w_down, preferred_element_type=jnp.float32)
    sig = jax.nn.sigmoid(pre)
    d_pre = (d_hidden * sig * (1.0 + pre * (1.0 - sig))).astype(jnp.bfloat16)
    return jnp.einsum("scf,df->scd", d_pre, w_up, preferred_element_type=jnp.float32).astype(
        jnp.bfloat16
    )


def shards(tokens, gates, routes, cotangent, up_weight, down_weight):
    w_up = up_weight[0]
    w_down = down_weight[0]
    tok_dev, width = tokens.shape
    top = routes.shape[1]
    ff_width = w_up.shape[1]
    senders = lax.axis_size("expert")
    experts = senders * up_weight.shape[0]
    capacity = max(2, min(tok_dev, 3 * tok_dev * top // (2 * experts)))
    owners = jnp.arange(senders, dtype=jnp.int32)
    route_blocks = jnp.broadcast_to(routes[None], (senders, tok_dev, top))
    gate_blocks = jnp.broadcast_to(gates[None], (senders, tok_dev, top))
    placing, slot_gates = slot_tables(route_blocks, gate_blocks, owners, capacity)
    rows = jnp.einsum("sct,td->scd", placing, tokens, preferred_element_type=jnp.float32).astype(
        jnp.bfloat16
    )
    arrived = lax.all_to_all(rows, "expert", split_axis=0, concat_axis=0, tiled=True)
    arrived_gates = lax.all_to_all(
        slot_gates.astype(jnp.bfloat16), "expert", split_axis=0, concat_axis=0, tiled=True
    )
    contrib, pre_part, hidden_part = expert_forward(
        arrived, arrived_gates.astype(jnp.float32), w_up, w_down
    )
    returned_part = lax.all_to_all(contrib, "expert", split_axis=0, concat_axis=0, tiled=True)
    mixed = jnp.einsum(
        "sct,scd->td", placing, returned_part, preferred_element_type=jnp.float32
    ).astype(jnp.bfloat16)
    slot_cot = jnp.einsum(
        "sct,td->scd", placing, cotangent, preferred_element_type=jnp.float32
    ).astype(jnp.bfloat16)
    outgoing = (slot_gates[..., None] * slot_cot.astype(jnp.float32)).astype(jnp.bfloat16)
    scaled = lax.all_to_all(outgoing, "expert", split_axis=0, concat_axis=0, tiled=True)
    d_rows = expert_backward(scaled, pre_part, w_up, w_down)
    came_back = lax.all_to_all(d_rows, "expert", split_axis=0, concat_axis=0, tiled=True)
    grad_tokens = jnp.einsum(
        "sct,scd->td", placing, came_back, preferred_element_type=jnp.float32
    ).astype(jnp.bfloat16)
    window_ff = ff_width // 2
    window_d = width // 2
    flat_hidden = hidden_part.reshape(-1, ff_width)[:, :window_ff]
    flat_scaled = scaled.reshape(-1, width)[:, :window_d]
    grad_down = lax.psum_scatter(
        lax.dot_general(
            flat_hidden, flat_scaled, (((0,), (0,)), ((), ())), preferred_element_type=jnp.float32
        ),
        "dp",
        scatter_dimension=0,
        tiled=True,
    )
    return (mixed, grad_tokens, grad_down[None])


def solution(mesh):
    chain = mesh.shape["dp"] == 8 and mesh.shape["expert"] == N
    return jax.shard_map(
        fused if chain else shards,
        mesh=mesh,
        in_specs=(
            P(("dp", "expert"), None),
            P(("dp", "expert"), None),
            P(("dp", "expert"), None),
            P(("dp", "expert"), None),
            P("expert", None, None),
            P("expert", None, None),
        ),
        out_specs=(P(("dp", "expert"), None), P(("dp", "expert"), None), P("expert", "dp", None)),
        check_vma=False,
    )
```

```python
import functools

import jax
import jax.numpy as jnp
from jax import lax
from jax.experimental import pallas as pl
from jax.experimental.pallas import tpu as pltpu
from jax.sharding import PartitionSpec as P

F32, BF16 = jnp.float32, jnp.bfloat16
N = 4
CH = 4
WINDOW = 4
MESH = pl.DeviceIdType.MESH


def dot(a, b, ca, cb):
    return lax.dot_general(a, b, (((ca,), (cb,)), ((), ())), preferred_element_type=F32)


def layer_kernel(
    tok, gates, routes, cot, wu, wd,
    mixed, gtok, gdown,
    X, G, SC, Y, R, WU, WD, WG, pre, dh, hid, dpre, GD, S1, R1, S2, R2,
    loc, ag_s, ag_r, rs_s, rs_r, g_s, g_r, p1_s, p1_r, p2_s, p2_r,
):
    T = tok.shape[0]
    W = X.shape[2]
    sh = gdown.shape[0]
    hw = GD.shape[0]
    cols = [slice(c * W, (c + 1) * W) for c in range(CH)]
    z = lax.axis_index("expert")
    p = lax.axis_index("dp")
    core, chip = lax.rem(p, 2), lax.div(p, 2)
    cx, cy = lax.rem(chip, 2), lax.div(chip, 2)
    mates = [chip, (1 - cx) + 2 * cy, cx + 2 * (1 - cy), (1 - cx) + 2 * (1 - cy)]
    other = 2 * chip + 1 - core

    def rows(s):
        return pl.ds(s * T, T)

    def here(fn):
        for k in range(N):
            pl.when(z == k)(functools.partial(fn, k))

    own = pl.ds(pl.multiple_of(z * T, T), T)
    locals_ = {}
    for c in range(CH):
        locals_["x", c] = pltpu.make_async_copy(tok.at[:, pl.ds(c * W, W)], X.at[c, own], loc.at[0, c])
        locals_["g", c] = pltpu.make_async_copy(cot.at[:, pl.ds(c * W, W)], G.at[c, own], loc.at[1, c])
        locals_["u", c] = pltpu.make_async_copy(wu.at[0, pl.ds(c * W, W)], WU.at[c], loc.at[2, c])
        locals_["d", c] = pltpu.make_async_copy(wd.at[0, :, pl.ds(c * W, W)], WD.at[c], loc.at[3, c])
    for name in "xgud":
        for c in range(CH):
            locals_[name, c].start()

    barrier = pltpu.get_barrier_semaphore()
    for d in range(1, N):
        pl.semaphore_signal(barrier, inc=1, device_id={"expert": lax.rem(z + d, N)}, device_id_type=MESH)
    for peer in [other] + [2 * m + core for m in mates[1:]]:
        pl.semaphore_signal(barrier, inc=1, device_id={"dp": peer}, device_id_type=MESH)

    expert = lax.broadcasted_iota(jnp.int32, (WG.shape[1], T), 0)
    table = jnp.zeros(expert.shape, F32)
    for j in range(routes.shape[0]):
        table += jnp.where(routes[j : j + 1, :] == expert, gates[j : j + 1, :].astype(F32), 0.0)
    eye = lax.broadcasted_iota(jnp.int32, (T, T), 0) == lax.broadcasted_iota(jnp.int32, (T, T), 1)
    WG[own, :] = dot(eye.astype(F32).astype(BF16), table.astype(BF16), 1, 1).astype(BF16)
    for c in range(CH):
        locals_["x", c].wait()
    pl.semaphore_wait(barrier, 7)

    def ag(ph, c, s, k, step):
        buf = (X, G)[ph].at[c, rows(s)]
        return pltpu.make_async_remote_copy(
            src_ref=buf, dst_ref=buf,
            send_sem=ag_s.at[ph, c, s, (step + 1) // 2], recv_sem=ag_r.at[ph, c, s],
            device_id={"expert": k + step}, device_id_type=MESH,
        )

    def ag_sends(ph, c, k, h):
        if h == 0:
            return [ag(ph, c, k, k, st) for st in (1, -1) if 0 <= k + st < N]
        out = []
        for st in (1, -1):
            if 0 <= k - st * h < N and 0 <= k + st < N:
                out.append(ag(ph, c, k - st * h, k, st))
        return out

    def ag_step(ph, c, h):
        def fn(k):
            for st in (1, -1):
                s = k - st * h
                if 0 <= s < N:
                    ag(ph, c, s, k, st).wait_recv()
                    if 0 <= k + st < N:
                        ag(ph, c, s, k, st).start()

        here(fn)

    def ag_open(ph):
        def fn(k):
            for c in range(CH):
                for cp in ag_sends(ph, c, k, 0):
                    cp.start()

        here(fn)

    def rs(ph, c, s, k):
        step = 1 if s > k else -1
        slot = s + 1 if step == 1 else s
        return pltpu.make_async_remote_copy(
            src_ref=Y.at[ph, c, rows(s)], dst_ref=R.at[ph, c, rows(slot)],
            send_sem=rs_s.at[ph, c, s], recv_sem=rs_r.at[ph, c, slot],
            device_id={"expert": k + step}, device_id_type=MESH,
        )

    def rs_arrived(ph, c, s, k, step):
        slot = s + 1 if step == 1 else s
        pltpu.make_async_remote_copy(
            src_ref=Y.at[ph, c, rows(s)], dst_ref=R.at[ph, c, rows(slot)],
            send_sem=rs_s.at[ph, c, s], recv_sem=rs_r.at[ph, c, slot],
            device_id={"expert": k - step}, device_id_type=MESH,
        ).wait_recv()
        return R[ph, c, rows(slot), :].astype(F32)

    def rs_open(ph, first, last):
        def fn(k, targets):
            sent = [rs(ph, c, s, k) for s in targets for c in range(CH)]
            for i in range(first, last):
                if i >= WINDOW:
                    sent[i - WINDOW].wait_send()
                sent[i].start()

        pl.when(z == 0)(functools.partial(fn, 0, list(range(N - 1, 0, -1))))
        pl.when(z == N - 1)(functools.partial(fn, N - 1, list(range(N - 1))))

    def rs_left(k):
        targets = list(range(N - 1, 0, -1)) if k == 0 else [s for s in range(N) if s != k]
        every = [(s, c) for s in targets for c in range(CH)]
        return every[-WINDOW:] if k in (0, N - 1) else every

    def rs_pass(ph):
        def add(c, s, k, step):
            got = rs_arrived(ph, c, s, k, step)
            Y[ph, c, rows(s), :] = (Y[ph, c, rows(s), :].astype(F32) + got).astype(BF16)
            rs(ph, c, s, k).start()

        def fn(k, step, far, near, back_to):
            for c in range(CH):
                add(c, far, k, step)
            for c in range(CH):
                add(c, near, k, step)
                add(c, back_to, k, -step)

        pl.when(z == 1)(functools.partial(fn, 1, 1, 3, 2, 0))
        pl.when(z == 2)(functools.partial(fn, 2, -1, 0, 1, 3))

    def rs_close(ph, c):
        out = (mixed, gtok)[ph]

        def fn(k):
            total = Y[ph, c, rows(k), :].astype(F32)
            if k > 0:
                total += rs_arrived(ph, c, k, k, 1)
            if k < N - 1:
                total += rs_arrived(ph, c, k, k, -1)
            out[:, cols[c]] = total.astype(BF16)

        here(fn)

    def gate(k, s):
        return pltpu.make_async_remote_copy(
            src_ref=WG.at[rows(k)], dst_ref=WG.at[rows(k)],
            send_sem=g_s.at[s], recv_sem=g_r.at[k],
            device_id={"expert": s}, device_id_type=MESH,
        )

    ag_open(0)

    def gate_open(k):
        for s in range(N):
            if s != k:
                gate(k, s).start()

    here(gate_open)

    def up(c):
        locals_["u", c].wait()
        part = dot(X[c], WU[c], 1, 0)
        pre[...] = part if c == 0 else pre[...] + part

    for t in range(CH + 2):
        if t < CH:
            ag_step(0, t, 1)
        if 0 <= t - 1 < CH:
            ag_step(0, t - 1, 2)
        if t == CH:
            for c in range(CH):
                locals_["g", c].wait()
            ag_open(1)
        if 0 <= t - 2 < CH:
            ag_step(0, t - 2, 3)
            up(t - 2)

    def gate_close(k):
        for s in range(N):
            if s != k:
                gate(s, k).wait_recv()

    here(gate_close)
    wide = WG[...].astype(F32)
    gcol = jnp.sum(
        jnp.where(lax.broadcasted_iota(jnp.int32, wide.shape, 1) == z, wide, 0.0), axis=1, keepdims=True
    )
    v = pre[...]
    hid[...] = (v / (1.0 + jnp.exp(-v))).astype(BF16)

    def down(c):
        locals_["d", c].wait()
        Y[0, c] = (gcol * dot(hid[...], WD[c], 1, 0)).astype(BF16)

    def back(c):
        SC[c] = (gcol * G[c].astype(F32)).astype(BF16)
        part = dot(SC[c], WD[c], 1, 1)
        dh[...] = part if c == 0 else dh[...] + part

    def plane1(m):
        return pltpu.make_async_remote_copy(
            src_ref=S1.at[m], dst_ref=R1.at[m], send_sem=p1_s.at[m], recv_sem=p1_r.at[m],
            device_id={"dp": other}, device_id_type=MESH,
        )

    def plane2(d):
        return pltpu.make_async_remote_copy(
            src_ref=S2.at[d - 1], dst_ref=R2.at[d - 1], send_sem=p2_s.at[d - 1], recv_sem=p2_r.at[d - 1],
            device_id={"dp": 2 * mates[d] + core}, device_id_type=MESH,
        )

    def shard(i):
        return pl.ds(pl.multiple_of(i * sh, 16), sh)

    def grads():
        half = hid[:, :hw]
        for c in range(CH // 2):
            GD[:, cols[c]] = dot(half, SC[c], 0, 0)
        for m in range(4):
            S1[m] = GD[shard(2 * m + 1 - core), :].astype(BF16)
            plane1(m).start()

    for c in range(CH):
        down(c)
        rs_open(0, c, c + 1)
    for c in range(CH):
        ag_step(1, c, 1)
    rs_open(0, CH, 2 * CH)
    for c in range(CH):
        ag_step(1, c, 2)
    for c in range(CH):
        ag_step(1, c, 3)
        back(c)
        rs_open(0, 2 * CH + c, 2 * CH + c + 1)

    sig = 1.0 / (1.0 + jnp.exp(-pre[...]))
    dpre[...] = (dh[...] * sig * (1.0 + pre[...] * (1.0 - sig))).astype(BF16)
    for c in range(CH):
        Y[1, c] = dot(dpre[...], WU[c], 1, 1).astype(BF16)
        rs_open(1, c, c + 1)
    grads()
    rs_open(1, CH, 2 * CH)
    for m in range(4):
        plane1(m).wait_recv()
    for d in range(1, 4):
        S2[d - 1] = (GD[shard(2 * mates[d] + core), :] + R1[mates[d]].astype(F32)).astype(BF16)
        plane2(d).start()
    rs_open(1, 2 * CH, 3 * CH)
    rs_pass(0)
    rs_pass(1)
    for c in range(CH):
        rs_close(0, c)
    total = GD[shard(2 * chip + core), :] + R1[chip].astype(F32)
    for d in range(1, 4):
        plane2(d).wait_recv()
        total += R2[d - 1].astype(F32)
    gdown[...] = total
    for c in range(CH):
        rs_close(1, c)

    def drain(k):
        for ph in range(2):
            for c in range(CH):
                for h in range(N - 1):
                    for cp in ag_sends(ph, c, k, h):
                        cp.wait_send()
            for s, c in rs_left(k):
                rs(ph, c, s, k).wait_send()
        for s in range(N):
            if s != k:
                gate(k, s).wait_send()

    here(drain)
    for m in range(4):
        plane1(m).wait_send()
    for d in range(1, 4):
        plane2(d).wait_send()


def fused(tokens, gates, routes, cotangent, up_weight, down_weight):
    T, D = tokens.shape
    FF = up_weight.shape[2]
    W = D // CH
    hw, dw = FF // 2, D // 2
    sh = hw // 8
    A = N * T
    dma = pltpu.SemaphoreType.DMA
    anyspace = pl.BlockSpec(memory_space=pl.ANY)
    vmem = pl.BlockSpec(memory_space=pltpu.VMEM)
    mixed, gtok, gdown = pl.pallas_call(
        layer_kernel,
        out_shape=(
            jax.ShapeDtypeStruct((T, D), BF16),
            jax.ShapeDtypeStruct((T, D), BF16),
            jax.ShapeDtypeStruct((sh, dw), F32),
        ),
        in_specs=[anyspace, vmem, vmem, anyspace, anyspace, anyspace],
        out_specs=(vmem, vmem, vmem),
        scratch_shapes=[
            pltpu.VMEM((CH, A, W), BF16),
            pltpu.VMEM((CH, A, W), BF16),
            pltpu.VMEM((CH, A, W), BF16),
            pltpu.VMEM((2, CH, A, W), BF16),
            pltpu.VMEM((2, CH, A + T, W), BF16),
            pltpu.VMEM((CH, W, FF), BF16),
            pltpu.VMEM((CH, FF, W), BF16),
            pltpu.VMEM((A, 128), BF16),
            pltpu.VMEM((A, FF), F32),
            pltpu.VMEM((A, FF), F32),
            pltpu.VMEM((A, FF), BF16),
            pltpu.VMEM((A, FF), BF16),
            pltpu.VMEM((hw, dw), F32),
            pltpu.VMEM((4, sh, dw), BF16),
            pltpu.VMEM((4, sh, dw), BF16),
            pltpu.VMEM((3, sh, dw), BF16),
            pltpu.VMEM((3, sh, dw), BF16),
            dma((4, CH)),
            dma((2, CH, N, 2)),
            dma((2, CH, N)),
            dma((2, CH, N)),
            dma((2, CH, N + 1)),
            dma((N,)),
            dma((N,)),
            dma((4,)),
            dma((4,)),
            dma((3,)),
            dma((3,)),
        ],
        compiler_params=pltpu.CompilerParams(
            collective_id=0, has_side_effects=True, vmem_limit_bytes=60 * 1024 * 1024
        ),
    )(tokens, gates.T, routes.T, cotangent, up_weight, down_weight)
    return (mixed, gtok, gdown[None])


def slot_tables(route_blocks, gate_blocks, owners, capacity):
    matches = route_blocks == owners[:, None, None]
    chosen = jnp.sum(matches.astype(jnp.int32), axis=2)
    weights = jnp.sum(jnp.where(matches, gate_blocks.astype(jnp.float32), jnp.float32(0.0)), axis=2)
    ranks = jnp.cumsum(chosen, axis=1) - 1
    positions = jnp.arange(capacity, dtype=jnp.int32)
    placed = (chosen[:, None, :] == 1) & (ranks[:, None, :] == positions[None, :, None])
    placing = placed.astype(jnp.bfloat16)
    slot_gates = jnp.einsum(
        "bct,bt->bc", placing, weights.astype(jnp.bfloat16), preferred_element_type=jnp.float32
    )
    return (placing, slot_gates)


def expert_forward(rows, slot_gates, w_up, w_down):
    pre = jnp.einsum("scd,df->scf", rows, w_up, preferred_element_type=jnp.float32)
    hidden = jax.nn.silu(pre).astype(jnp.bfloat16)
    outputs = jnp.einsum("scf,fd->scd", hidden, w_down, preferred_element_type=jnp.float32)
    contrib = (slot_gates[..., None] * outputs).astype(jnp.bfloat16)
    return (contrib, pre, hidden)


def expert_backward(scaled, pre, w_up, w_down):
    d_hidden = jnp.einsum("scd,fd->scf", scaled, w_down, preferred_element_type=jnp.float32)
    sig = jax.nn.sigmoid(pre)
    d_pre = (d_hidden * sig * (1.0 + pre * (1.0 - sig))).astype(jnp.bfloat16)
    return jnp.einsum("scf,df->scd", d_pre, w_up, preferred_element_type=jnp.float32).astype(
        jnp.bfloat16
    )


def shards(tokens, gates, routes, cotangent, up_weight, down_weight):
    w_up = up_weight[0]
    w_down = down_weight[0]
    tok_dev, width = tokens.shape
    top = routes.shape[1]
    ff_width = w_up.shape[1]
    senders = lax.axis_size("expert")
    experts = senders * up_weight.shape[0]
    capacity = max(2, min(tok_dev, 3 * tok_dev * top // (2 * experts)))
    owners = jnp.arange(senders, dtype=jnp.int32)
    route_blocks = jnp.broadcast_to(routes[None], (senders, tok_dev, top))
    gate_blocks = jnp.broadcast_to(gates[None], (senders, tok_dev, top))
    placing, slot_gates = slot_tables(route_blocks, gate_blocks, owners, capacity)
    rows = jnp.einsum("sct,td->scd", placing, tokens, preferred_element_type=jnp.float32).astype(
        jnp.bfloat16
    )
    arrived = lax.all_to_all(rows, "expert", split_axis=0, concat_axis=0, tiled=True)
    arrived_gates = lax.all_to_all(
        slot_gates.astype(jnp.bfloat16), "expert", split_axis=0, concat_axis=0, tiled=True
    )
    contrib, pre_part, hidden_part = expert_forward(
        arrived, arrived_gates.astype(jnp.float32), w_up, w_down
    )
    returned_part = lax.all_to_all(contrib, "expert", split_axis=0, concat_axis=0, tiled=True)
    mixed = jnp.einsum(
        "sct,scd->td", placing, returned_part, preferred_element_type=jnp.float32
    ).astype(jnp.bfloat16)
    slot_cot = jnp.einsum(
        "sct,td->scd", placing, cotangent, preferred_element_type=jnp.float32
    ).astype(jnp.bfloat16)
    outgoing = (slot_gates[..., None] * slot_cot.astype(jnp.float32)).astype(jnp.bfloat16)
    scaled = lax.all_to_all(outgoing, "expert", split_axis=0, concat_axis=0, tiled=True)
    d_rows = expert_backward(scaled, pre_part, w_up, w_down)
    came_back = lax.all_to_all(d_rows, "expert", split_axis=0, concat_axis=0, tiled=True)
    grad_tokens = jnp.einsum(
        "sct,scd->td", placing, came_back, preferred_element_type=jnp.float32
    ).astype(jnp.bfloat16)
    window_ff = ff_width // 2
    window_d = width // 2
    flat_hidden = hidden_part.reshape(-1, ff_width)[:, :window_ff]
    flat_scaled = scaled.reshape(-1, width)[:, :window_d]
    grad_down = lax.psum_scatter(
        lax.dot_general(
            flat_hidden, flat_scaled, (((0,), (0,)), ((), ())), preferred_element_type=jnp.float32
        ),
        "dp",
        scatter_dimension=0,
        tiled=True,
    )
    return (mixed, grad_tokens, grad_down[None])


def solution(mesh):
    chain = mesh.shape["dp"] == 8 and mesh.shape["expert"] == N
    return jax.shard_map(
        fused if chain else shards,
        mesh=mesh,
        in_specs=(
            P(("dp", "expert"), None),
            P(("dp", "expert"), None),
            P(("dp", "expert"), None),
            P(("dp", "expert"), None),
            P("expert", None, None),
            P("expert", None, None),
        ),
        out_specs=(P(("dp", "expert"), None), P(("dp", "expert"), None), P("expert", "dp", None)),
        check_vma=False,
    )
```

```python
import functools

import jax
import jax.numpy as jnp
from jax import lax
from jax.experimental import pallas as pl
from jax.experimental.pallas import tpu as pltpu
from jax.sharding import PartitionSpec as P

F32, BF16 = jnp.float32, jnp.bfloat16
N = 4
CH = 4
WINDOW = 4
MESH = pl.DeviceIdType.MESH


def dot(a, b, ca, cb):
    return lax.dot_general(a, b, (((ca,), (cb,)), ((), ())), preferred_element_type=F32)


def layer_kernel(
    tok, gates, routes, cot, wu, wd,
    mixed, gtok, gdown,
    X, G, SC, Y, R, WU, WD, WG, pre, dh, hid, dpre, GD, S1, R1, S2, R2,
    loc, ag_s, ag_r, rs_s, rs_r, g_s, g_r, p1_s, p1_r, p2_s, p2_r,
):
    T = tok.shape[0]
    W = X.shape[2]
    sh = gdown.shape[0]
    hw = GD.shape[0]
    cols = [slice(c * W, (c + 1) * W) for c in range(CH)]
    z = lax.axis_index("expert")
    p = lax.axis_index("dp")
    core, chip = lax.rem(p, 2), lax.div(p, 2)
    cx, cy = lax.rem(chip, 2), lax.div(chip, 2)
    mates = [chip, (1 - cx) + 2 * cy, cx + 2 * (1 - cy), (1 - cx) + 2 * (1 - cy)]
    other = 2 * chip + 1 - core

    def rows(s):
        return pl.ds(s * T, T)

    def here(fn):
        for k in range(N):
            pl.when(z == k)(functools.partial(fn, k))

    own = pl.ds(pl.multiple_of(z * T, T), T)
    locals_ = {}
    for c in range(CH):
        locals_["x", c] = pltpu.make_async_copy(tok.at[:, pl.ds(c * W, W)], X.at[c, own], loc.at[0, c])
        locals_["g", c] = pltpu.make_async_copy(cot.at[:, pl.ds(c * W, W)], G.at[c, own], loc.at[1, c])
        locals_["u", c] = pltpu.make_async_copy(wu.at[0, pl.ds(c * W, W)], WU.at[c], loc.at[2, c])
        locals_["d", c] = pltpu.make_async_copy(wd.at[0, :, pl.ds(c * W, W)], WD.at[c], loc.at[3, c])
    for name in "xgud":
        for c in range(CH):
            locals_[name, c].start()

    barrier = pltpu.get_barrier_semaphore()
    for d in range(1, N):
        pl.semaphore_signal(barrier, inc=1, device_id={"expert": lax.rem(z + d, N)}, device_id_type=MESH)
    for peer in [other] + [2 * m + core for m in mates[1:]]:
        pl.semaphore_signal(barrier, inc=1, device_id={"dp": peer}, device_id_type=MESH)

    expert = lax.broadcasted_iota(jnp.int32, (WG.shape[1], T), 0)
    table = jnp.zeros(expert.shape, F32)
    for j in range(routes.shape[0]):
        table += jnp.where(routes[j : j + 1, :] == expert, gates[j : j + 1, :].astype(F32), 0.0)
    eye = lax.broadcasted_iota(jnp.int32, (T, T), 0) == lax.broadcasted_iota(jnp.int32, (T, T), 1)
    WG[own, :] = dot(eye.astype(F32).astype(BF16), table.astype(BF16), 1, 1).astype(BF16)
    for c in range(CH):
        locals_["x", c].wait()
    pl.semaphore_wait(barrier, 7)

    def ag(ph, c, s, k, step):
        buf = (X, G)[ph].at[c, rows(s)]
        return pltpu.make_async_remote_copy(
            src_ref=buf, dst_ref=buf,
            send_sem=ag_s.at[ph, c, s, (step + 1) // 2], recv_sem=ag_r.at[ph, c, s],
            device_id={"expert": k + step}, device_id_type=MESH,
        )

    def ag_sends(ph, c, k, h):
        if h == 0:
            return [ag(ph, c, k, k, st) for st in (1, -1) if 0 <= k + st < N]
        out = []
        for st in (1, -1):
            if 0 <= k - st * h < N and 0 <= k + st < N:
                out.append(ag(ph, c, k - st * h, k, st))
        return out

    def ag_step(ph, c, h):
        def fn(k):
            for st in (1, -1):
                s = k - st * h
                if 0 <= s < N:
                    ag(ph, c, s, k, st).wait_recv()
                    if 0 <= k + st < N:
                        ag(ph, c, s, k, st).start()

        here(fn)

    def ag_open(ph):
        def fn(k):
            for c in range(CH):
                for cp in ag_sends(ph, c, k, 0):
                    cp.start()

        here(fn)

    def rs(ph, c, s, k):
        step = 1 if s > k else -1
        slot = s + 1 if step == 1 else s
        return pltpu.make_async_remote_copy(
            src_ref=Y.at[ph, c, rows(s)], dst_ref=R.at[ph, c, rows(slot)],
            send_sem=rs_s.at[ph, c, s], recv_sem=rs_r.at[ph, c, slot],
            device_id={"expert": k + step}, device_id_type=MESH,
        )

    def rs_arrived(ph, c, s, k, step):
        slot = s + 1 if step == 1 else s
        pltpu.make_async_remote_copy(
            src_ref=Y.at[ph, c, rows(s)], dst_ref=R.at[ph, c, rows(slot)],
            send_sem=rs_s.at[ph, c, s], recv_sem=rs_r.at[ph, c, slot],
            device_id={"expert": k - step}, device_id_type=MESH,
        ).wait_recv()
        return R[ph, c, rows(slot), :].astype(F32)

    def rs_open(ph, first, last):
        def fn(k, targets):
            sent = [rs(ph, c, s, k) for s in targets for c in range(CH)]
            for i in range(first, last):
                if i >= WINDOW:
                    sent[i - WINDOW].wait_send()
                sent[i].start()

        pl.when(z == 0)(functools.partial(fn, 0, list(range(N - 1, 0, -1))))
        pl.when(z == N - 1)(functools.partial(fn, N - 1, list(range(N - 1))))

    def rs_left(k):
        targets = list(range(N - 1, 0, -1)) if k == 0 else [s for s in range(N) if s != k]
        every = [(s, c) for s in targets for c in range(CH)]
        return every[-WINDOW:] if k in (0, N - 1) else every

    def rs_pass(ph):
        def add(c, s, k, step):
            got = rs_arrived(ph, c, s, k, step)
            Y[ph, c, rows(s), :] = (Y[ph, c, rows(s), :].astype(F32) + got).astype(BF16)
            rs(ph, c, s, k).start()

        def fn(k, step, far, near, back_to):
            for c in range(CH):
                add(c, far, k, step)
            for c in range(CH):
                add(c, near, k, step)
                add(c, back_to, k, -step)

        pl.when(z == 1)(functools.partial(fn, 1, 1, 3, 2, 0))
        pl.when(z == 2)(functools.partial(fn, 2, -1, 0, 1, 3))

    def rs_close(ph, c):
        out = (mixed, gtok)[ph]

        def fn(k):
            total = Y[ph, c, rows(k), :].astype(F32)
            if k > 0:
                total += rs_arrived(ph, c, k, k, 1)
            if k < N - 1:
                total += rs_arrived(ph, c, k, k, -1)
            out[:, cols[c]] = total.astype(BF16)

        here(fn)

    def gate(k, s):
        return pltpu.make_async_remote_copy(
            src_ref=WG.at[rows(k)], dst_ref=WG.at[rows(k)],
            send_sem=g_s.at[s], recv_sem=g_r.at[k],
            device_id={"expert": s}, device_id_type=MESH,
        )

    ag_open(0)

    def gate_open(k):
        for s in range(N):
            if s != k:
                gate(k, s).start()

    here(gate_open)

    def up(c):
        locals_["u", c].wait()
        part = dot(X[c], WU[c], 1, 0)
        pre[...] = part if c == 0 else pre[...] + part

    for t in range(CH + 2):
        if t < CH:
            ag_step(0, t, 1)
        if 0 <= t - 1 < CH:
            ag_step(0, t - 1, 2)
        if t == CH:
            for c in range(CH):
                locals_["g", c].wait()
            ag_open(1)
        if 0 <= t - 2 < CH:
            ag_step(0, t - 2, 3)
            up(t - 2)

    def gate_close(k):
        for s in range(N):
            if s != k:
                gate(s, k).wait_recv()

    here(gate_close)
    wide = WG[...].astype(F32)
    gcol = jnp.sum(
        jnp.where(lax.broadcasted_iota(jnp.int32, wide.shape, 1) == z, wide, 0.0), axis=1, keepdims=True
    )
    v = pre[...]
    hid[...] = (v / (1.0 + jnp.exp(-v))).astype(BF16)

    def down(c):
        locals_["d", c].wait()
        Y[0, c] = (gcol * dot(hid[...], WD[c], 1, 0)).astype(BF16)

    def back(c):
        SC[c] = (gcol * G[c].astype(F32)).astype(BF16)
        part = dot(SC[c], WD[c], 1, 1)
        dh[...] = part if c == 0 else dh[...] + part

    def plane1(m):
        return pltpu.make_async_remote_copy(
            src_ref=S1.at[m], dst_ref=R1.at[m], send_sem=p1_s.at[m], recv_sem=p1_r.at[m],
            device_id={"dp": other}, device_id_type=MESH,
        )

    def plane2(d):
        return pltpu.make_async_remote_copy(
            src_ref=S2.at[d - 1], dst_ref=R2.at[d - 1], send_sem=p2_s.at[d - 1], recv_sem=p2_r.at[d - 1],
            device_id={"dp": 2 * mates[d] + core}, device_id_type=MESH,
        )

    def shard(i):
        return pl.ds(pl.multiple_of(i * sh, 16), sh)

    def grads():
        half = hid[:, :hw]
        for c in range(CH // 2):
            GD[:, cols[c]] = dot(half, SC[c], 0, 0)
        for m in range(4):
            S1[m] = GD[shard(2 * m + 1 - core), :].astype(BF16)
            plane1(m).start()

    for c in range(CH):
        down(c)
    rs_open(0, 0, 3 * CH)
    for c in range(CH):
        ag_step(1, c, 1)
    for c in range(CH):
        ag_step(1, c, 2)
    for c in range(CH):
        ag_step(1, c, 3)
        back(c)
        if c == CH // 2 - 1:
            grads()

    sig = 1.0 / (1.0 + jnp.exp(-pre[...]))
    dpre[...] = (dh[...] * sig * (1.0 + pre[...] * (1.0 - sig))).astype(BF16)
    for c in range(CH):
        Y[1, c] = dot(dpre[...], WU[c], 1, 1).astype(BF16)
        rs_open(1, c, c + 1)
    for m in range(4):
        plane1(m).wait_recv()
    for d in range(1, 4):
        S2[d - 1] = (GD[shard(2 * mates[d] + core), :] + R1[mates[d]].astype(F32)).astype(BF16)
        plane2(d).start()
    rs_open(1, CH, 3 * CH)
    rs_pass(0)
    rs_pass(1)
    for c in range(CH):
        rs_close(0, c)
    total = GD[shard(2 * chip + core), :] + R1[chip].astype(F32)
    for d in range(1, 4):
        plane2(d).wait_recv()
        total += R2[d - 1].astype(F32)
    gdown[...] = total
    for c in range(CH):
        rs_close(1, c)

    def drain(k):
        for ph in range(2):
            for c in range(CH):
                for h in range(N - 1):
                    for cp in ag_sends(ph, c, k, h):
                        cp.wait_send()
            for s, c in rs_left(k):
                rs(ph, c, s, k).wait_send()
        for s in range(N):
            if s != k:
                gate(k, s).wait_send()

    here(drain)
    for m in range(4):
        plane1(m).wait_send()
    for d in range(1, 4):
        plane2(d).wait_send()


def hand_over(a, b, c, a_out, b_out, c_out, sem):
    copies = [
        pltpu.make_async_copy(src, dst, sem.at[i])
        for i, (src, dst) in enumerate(((a, a_out), (b, b_out), (c, c_out)))
    ]
    for cp in copies:
        cp.start()
    for cp in copies:
        cp.wait()


def fused(tokens, gates, routes, cotangent, up_weight, down_weight):
    T, D = tokens.shape
    FF = up_weight.shape[2]
    W = D // CH
    hw, dw = FF // 2, D // 2
    sh = hw // 8
    A = N * T
    dma = pltpu.SemaphoreType.DMA
    anyspace = pl.BlockSpec(memory_space=pl.ANY)
    vmem = pl.BlockSpec(memory_space=pltpu.VMEM)
    mixed, gtok, gdown = pl.pallas_call(
        layer_kernel,
        out_shape=(
            jax.ShapeDtypeStruct((T, D), BF16),
            jax.ShapeDtypeStruct((T, D), BF16),
            jax.ShapeDtypeStruct((sh, dw), F32),
        ),
        in_specs=[anyspace, vmem, vmem, anyspace, anyspace, anyspace],
        out_specs=(vmem, vmem, vmem),
        scratch_shapes=[
            pltpu.VMEM((CH, A, W), BF16),
            pltpu.VMEM((CH, A, W), BF16),
            pltpu.VMEM((CH, A, W), BF16),
            pltpu.VMEM((2, CH, A, W), BF16),
            pltpu.VMEM((2, CH, A + T, W), BF16),
            pltpu.VMEM((CH, W, FF), BF16),
            pltpu.VMEM((CH, FF, W), BF16),
            pltpu.VMEM((A, 128), BF16),
            pltpu.VMEM((A, FF), F32),
            pltpu.VMEM((A, FF), F32),
            pltpu.VMEM((A, FF), BF16),
            pltpu.VMEM((A, FF), BF16),
            pltpu.VMEM((hw, dw), F32),
            pltpu.VMEM((4, sh, dw), BF16),
            pltpu.VMEM((4, sh, dw), BF16),
            pltpu.VMEM((3, sh, dw), BF16),
            pltpu.VMEM((3, sh, dw), BF16),
            dma((4, CH)),
            dma((2, CH, N, 2)),
            dma((2, CH, N)),
            dma((2, CH, N)),
            dma((2, CH, N + 1)),
            dma((N,)),
            dma((N,)),
            dma((4,)),
            dma((4,)),
            dma((3,)),
            dma((3,)),
        ],
        compiler_params=pltpu.CompilerParams(
            collective_id=0, has_side_effects=True, vmem_limit_bytes=60 * 1024 * 1024
        ),
    )(tokens, gates.T, routes.T, cotangent, up_weight, down_weight)
    results = (mixed, gtok, gdown)
    mixed, gtok, gdown = pl.pallas_call(
        hand_over,
        out_shape=tuple(jax.ShapeDtypeStruct(r.shape, r.dtype) for r in results),
        in_specs=[anyspace] * 3,
        out_specs=(anyspace,) * 3,
        scratch_shapes=[dma((3,))],
    )(*results)
    return (mixed, gtok, gdown[None])


def slot_tables(route_blocks, gate_blocks, owners, capacity):
    matches = route_blocks == owners[:, None, None]
    chosen = jnp.sum(matches.astype(jnp.int32), axis=2)
    weights = jnp.sum(jnp.where(matches, gate_blocks.astype(jnp.float32), jnp.float32(0.0)), axis=2)
    ranks = jnp.cumsum(chosen, axis=1) - 1
    positions = jnp.arange(capacity, dtype=jnp.int32)
    placed = (chosen[:, None, :] == 1) & (ranks[:, None, :] == positions[None, :, None])
    placing = placed.astype(jnp.bfloat16)
    slot_gates = jnp.einsum(
        "bct,bt->bc", placing, weights.astype(jnp.bfloat16), preferred_element_type=jnp.float32
    )
    return (placing, slot_gates)


def expert_forward(rows, slot_gates, w_up, w_down):
    pre = jnp.einsum("scd,df->scf", rows, w_up, preferred_element_type=jnp.float32)
    hidden = jax.nn.silu(pre).astype(jnp.bfloat16)
    outputs = jnp.einsum("scf,fd->scd", hidden, w_down, preferred_element_type=jnp.float32)
    contrib = (slot_gates[..., None] * outputs).astype(jnp.bfloat16)
    return (contrib, pre, hidden)


def expert_backward(scaled, pre, w_up, w_down):
    d_hidden = jnp.einsum("scd,fd->scf", scaled, w_down, preferred_element_type=jnp.float32)
    sig = jax.nn.sigmoid(pre)
    d_pre = (d_hidden * sig * (1.0 + pre * (1.0 - sig))).astype(jnp.bfloat16)
    return jnp.einsum("scf,df->scd", d_pre, w_up, preferred_element_type=jnp.float32).astype(
        jnp.bfloat16
    )


def shards(tokens, gates, routes, cotangent, up_weight, down_weight):
    w_up = up_weight[0]
    w_down = down_weight[0]
    tok_dev, width = tokens.shape
    top = routes.shape[1]
    ff_width = w_up.shape[1]
    senders = lax.axis_size("expert")
    experts = senders * up_weight.shape[0]
    capacity = max(2, min(tok_dev, 3 * tok_dev * top // (2 * experts)))
    owners = jnp.arange(senders, dtype=jnp.int32)
    route_blocks = jnp.broadcast_to(routes[None], (senders, tok_dev, top))
    gate_blocks = jnp.broadcast_to(gates[None], (senders, tok_dev, top))
    placing, slot_gates = slot_tables(route_blocks, gate_blocks, owners, capacity)
    rows = jnp.einsum("sct,td->scd", placing, tokens, preferred_element_type=jnp.float32).astype(
        jnp.bfloat16
    )
    arrived = lax.all_to_all(rows, "expert", split_axis=0, concat_axis=0, tiled=True)
    arrived_gates = lax.all_to_all(
        slot_gates.astype(jnp.bfloat16), "expert", split_axis=0, concat_axis=0, tiled=True
    )
    contrib, pre_part, hidden_part = expert_forward(
        arrived, arrived_gates.astype(jnp.float32), w_up, w_down
    )
    returned_part = lax.all_to_all(contrib, "expert", split_axis=0, concat_axis=0, tiled=True)
    mixed = jnp.einsum(
        "sct,scd->td", placing, returned_part, preferred_element_type=jnp.float32
    ).astype(jnp.bfloat16)
    slot_cot = jnp.einsum(
        "sct,td->scd", placing, cotangent, preferred_element_type=jnp.float32
    ).astype(jnp.bfloat16)
    outgoing = (slot_gates[..., None] * slot_cot.astype(jnp.float32)).astype(jnp.bfloat16)
    scaled = lax.all_to_all(outgoing, "expert", split_axis=0, concat_axis=0, tiled=True)
    d_rows = expert_backward(scaled, pre_part, w_up, w_down)
    came_back = lax.all_to_all(d_rows, "expert", split_axis=0, concat_axis=0, tiled=True)
    grad_tokens = jnp.einsum(
        "sct,scd->td", placing, came_back, preferred_element_type=jnp.float32
    ).astype(jnp.bfloat16)
    window_ff = ff_width // 2
    window_d = width // 2
    flat_hidden = hidden_part.reshape(-1, ff_width)[:, :window_ff]
    flat_scaled = scaled.reshape(-1, width)[:, :window_d]
    grad_down = lax.psum_scatter(
        lax.dot_general(
            flat_hidden, flat_scaled, (((0,), (0,)), ((), ())), preferred_element_type=jnp.float32
        ),
        "dp",
        scatter_dimension=0,
        tiled=True,
    )
    return (mixed, grad_tokens, grad_down[None])


def solution(mesh):
    chain = mesh.shape["dp"] == 8 and mesh.shape["expert"] == N
    return jax.shard_map(
        fused if chain else shards,
        mesh=mesh,
        in_specs=(
            P(("dp", "expert"), None),
            P(("dp", "expert"), None),
            P(("dp", "expert"), None),
            P(("dp", "expert"), None),
            P("expert", None, None),
            P("expert", None, None),
        ),
        out_specs=(P(("dp", "expert"), None), P(("dp", "expert"), None), P("expert", "dp", None)),
        check_vma=False,
    )
```
